32 devices in a mesh: rows: 2 (over x), specs: 16 (over z, y, core).
Axes of the slice: x: 2, y: 2, z: 4, core: 2. Of those that a mesh axis runs over, the one named last changes fastest.
Arguments:
- center: float32 [16, 512, 64], P('rows'), may hold values from -6 to 6
- radius: float32 [16, 512, 64], P('rows'), may hold values from 0.01 to 0.2
- conv_weight: float32 [3, 3, 64, 64], replicated, may hold values from -0.25 to 0.25
- conv_bias: float32 [64], replicated, may hold values from -3 to 3
- split_status: int32 [16, 512, 64], P('rows'), may hold values from 0 to 2
- out_coeffs: bfloat16 [128, 16, 512, 64], P('specs', 'rows'), may hold values from -6 to 6
- spec_ids: int32 [128], P('specs'), may hold values from 0 to 4095
- spec_offsets: float32 [4096], replicated, may hold values from -5 to 5
Outputs:
- input_coeffs: bfloat16 [128, 16, 512, 64], P('specs', 'rows')
- bounds: float32 [128], P('specs')
The draws below stay inside these ranges and needn't reach their ends.
All inputs are finite; a program needn't handle non-finite values.
Results may differ from the reference program's by a relative error of at most 0.0052.
Values may be sent and summed in bfloat16 or wider, within the bound.
A program may use at most 128 MiB of HBM per device.

```python
import math
import jax
import jax.numpy as jnp
from jax import lax

C = 64
W = 512
SPEC_TABLE = 4096
H = 16
SPECS = 128


def set_ends(values, stream_key, least, top_value):
    longest = values.shape.index(max(values.shape))
    spots = []
    for shift in (0, 1):
        where = [jax.random.randint(jax.random.fold_in(stream_key, axis), (), 0, length) for axis, length in enumerate(values.shape)]
        where[longest] = (where[longest] + shift) % values.shape[longest]
        spots.append(tuple(where))
    return values.at[spots[0]].set(least).at[spots[1]].set(top_value)


def level_of(key, extent, cuts, smallest, top_value):
    gain = 1.0
    for axis_at, parts in cuts:
        heights = jax.random.uniform(jax.random.fold_in(jax.random.fold_in(key, 6), axis_at), (parts,), jnp.float32, smallest / len(cuts), top_value / len(cuts))
        gain = gain * jnp.repeat(jnp.exp(heights), extent[axis_at] // parts).reshape((-1,) + (1,) * (len(extent) - 1 - axis_at))
    return gain


def noise(stream_key, shape, scale, most, split=(), dtype=jnp.bfloat16):
    loudness = level_of(stream_key, shape, split, -0.22, 0.18) if split else 1.0
    drawn = jax.random.normal(stream_key, shape, jnp.float32) * scale * loudness
    return jnp.minimum(jnp.maximum(drawn, -most), most).astype(dtype)


def setup_inputs(seed: int = 0) -> dict:
    streams_of = jax.random.split(jax.random.key(seed), 9)
    return {
        "center": noise(streams_of[0], (H, W, C), 1.0, 6.0, ((0, 2),), jnp.float32),
        "radius": jnp.clip(jnp.exp(math.log(0.2) - 2.9957323 * jax.random.uniform(streams_of[1], (H, W, C), jnp.float32) ** level_of(streams_of[1], (H, W, C), ((0, 2),), -0.2, 0.2)), 0.01, 0.2),
        "conv_weight": noise(streams_of[2], (3, 3, C, C), (9 * C) ** -0.5, 0.25, (), jnp.float32),
        "conv_bias": noise(streams_of[3], (C,), 0.5, 3.0, (), jnp.float32),
        "split_status": set_ends(jax.random.randint(streams_of[4], (H, W, C), 0, 3), jax.random.fold_in(streams_of[4], 1), 0, 2).astype(jnp.int32),
        "out_coeffs": noise(streams_of[5], (SPECS, H, W, C), 1.0, 6.0, ((0, 16), (1, 2))),
        "spec_ids": set_ends(jax.random.randint(streams_of[6], (SPECS,), 0, SPEC_TABLE), jax.random.fold_in(streams_of[6], 1), 0, SPEC_TABLE - 1).astype(jnp.int32),
        "spec_offsets": noise(streams_of[7], (SPEC_TABLE,), 1.0, 5.0, (), jnp.float32),
    }


def shifted_sum(padded, kernel):
    result = jnp.zeros((H, W, C), jnp.float32)
    for i in range(3):
        for j in range(3):
            result = result + jnp.einsum("hwc,cd->hwd", padded[i:i + H, j:j + W], kernel[i, j], precision=lax.Precision.HIGHEST)
    return result


def reference(center, radius, conv_weight, conv_bias, split_status, out_coeffs, spec_ids, spec_offsets):
    edges = ((1, 1), (1, 1), (0, 0))
    center_out = conv_bias + shifted_sum(jnp.pad(center, edges), conv_weight)
    radius_out = shifted_sum(jnp.pad(radius, edges), jnp.abs(conv_weight))
    upper_end = center_out + radius_out
    lower_end = center_out - radius_out
    spread = 2.0 * radius_out
    relaxed = jnp.minimum(jnp.maximum(upper_end, 0.0), spread) / spread
    slopes = jnp.where(split_status == 2, relaxed, jnp.where(split_status == 1, 1.0, 0.0)).astype(jnp.bfloat16)
    intercepts = jnp.where(split_status == 2, -relaxed * jnp.minimum(lower_end, 0.0), 0.0).astype(jnp.bfloat16)
    weight_low = conv_weight.astype(jnp.bfloat16).astype(jnp.float32)

    def one_spec(coeffs):
        coeff_full = coeffs.astype(jnp.float32)
        pre_coeffs = (coeff_full * slopes.astype(jnp.float32)).astype(jnp.bfloat16)
        pre_full = pre_coeffs.astype(jnp.float32)
        offset_sum = jnp.sum(jnp.minimum(coeff_full, 0.0) * intercepts.astype(jnp.float32)) + jnp.sum(pre_full * conv_bias)
        padded = jnp.pad(pre_full, edges)
        input_coeffs = jnp.zeros((H, W, C), jnp.float32)
        for i in range(3):
            for j in range(3):
                input_coeffs = input_coeffs + jnp.einsum("hwd,cd->hwc", padded[2 - i:2 - i + H, 2 - j:2 - j + W], weight_low[i, j])
        summed = jnp.sum(input_coeffs * center - jnp.abs(input_coeffs) * radius) + offset_sum
        return input_coeffs.astype(jnp.bfloat16), summed / (H * W)

    input_coeffs, bounds = lax.map(one_spec, out_coeffs)
    return input_coeffs, bounds + spec_offsets[spec_ids]
```

```python
import functools

import jax
import jax.numpy as jnp
from jax import lax
from jax.experimental import pallas as pl
from jax.experimental.pallas import tpu as pltpu
from jax.sharding import PartitionSpec as P

F32 = jnp.float32
BF16 = jnp.bfloat16
MESH = pl.DeviceIdType.MESH


def split2(value):
    high = value.astype(BF16)
    return high, (value - high.astype(F32)).astype(BF16)


def combine(first, middle, last):
    width = first.shape[1]
    rolled = pltpu.roll(first, 1, 1)
    lane = lax.broadcasted_iota(jnp.int32, (first.shape[0], 128), 1)
    rolled = jnp.concatenate(
        [jnp.where(lane == 0, 0.0, rolled[:, :128]), rolled[:, 128:]], axis=1
    )
    back = pltpu.roll(last, width - 1, 1)
    back = jnp.concatenate(
        [back[:, :-128], jnp.where(lane == 127, 0.0, back[:, -128:])], axis=1
    )
    return rolled + middle + back


def fold(value):
    rows, width = value.shape
    return jnp.sum(value.reshape(rows // 8, 8, width), axis=0)


def kernel(
    n_rows,
    center_hbm, radius_hbm, weight_ref, bias_ref, status_hbm, coeff_hbm, ids_ref, table_ref,
    out_ref, bounds_ref,
    center, radius, status, coeff,
    low_end, high_end, slopes, icept, edge_slopes,
    halo_box, halo_coeff, box_weight, rad_weight, back_weight, bias_col,
    acc, parts, table_vec,
    load_sem, coeff_sem, box_send, box_recv, pass_send, pass_recv,
    slope_send, slope_recv, spass_send, spass_recv, row_send, row_recv, part_send, part_recv,
):
    specs, rows, chans, cols = coeff.shape
    half = chans // 2
    me = lax.axis_index("rows")
    lane_dev = lax.axis_index("specs")
    core = lax.rem(lane_dev, 2)
    partner = lane_dev + 1 - 2 * core
    has_prev = me > 0
    has_next = me < n_rows - 1
    mine = pl.ds(pl.multiple_of(core * half, half), half)
    exists = (has_prev, has_next)
    sends = (has_next, has_prev)
    target = (me + 1, me - 1)
    edge = (rows - 1, 0)

    loads = [
        pltpu.make_async_copy(center_hbm, center.at[pl.ds(1, rows)], load_sem.at[0]),
        pltpu.make_async_copy(radius_hbm, radius.at[pl.ds(1, rows)], load_sem.at[1]),
        pltpu.make_async_copy(status_hbm, status, load_sem.at[2]),
    ]
    for copy in loads:
        copy.start()

    barrier = pltpu.get_barrier_semaphore()
    for step in range(1, n_rows):
        pl.semaphore_signal(
            barrier, inc=1, device_id={"rows": lax.rem(me + step, n_rows)}, device_id_type=MESH
        )
    pl.semaphore_signal(barrier, inc=1, device_id={"specs": partner}, device_id_type=MESH)
    pl.semaphore_wait(barrier, n_rows)

    def box_copy(d, a):
        return pltpu.make_async_remote_copy(
            src_ref=(center_hbm, radius_hbm)[a].at[edge[d], mine],
            dst_ref=halo_box.at[d, a, mine],
            send_sem=box_send.at[d, a],
            recv_sem=box_recv.at[d, a],
            device_id={"rows": target[d]},
            device_id_type=MESH,
        )

    def pass_copy(d):
        return pltpu.make_async_remote_copy(
            src_ref=halo_box.at[d, :, mine],
            dst_ref=halo_box.at[d, :, mine],
            send_sem=pass_send.at[d],
            recv_sem=pass_recv.at[d],
            device_id={"specs": partner},
            device_id_type=MESH,
        )

    def slope_copy(d):
        return pltpu.make_async_remote_copy(
            src_ref=slopes.at[edge[d], mine],
            dst_ref=edge_slopes.at[d, mine],
            send_sem=slope_send.at[d],
            recv_sem=slope_recv.at[d],
            device_id={"rows": target[d]},
            device_id_type=MESH,
        )

    def spass_copy(d):
        return pltpu.make_async_remote_copy(
            src_ref=edge_slopes.at[d, mine],
            dst_ref=edge_slopes.at[d, mine],
            send_sem=spass_send.at[d],
            recv_sem=spass_recv.at[d],
            device_id={"specs": partner},
            device_id_type=MESH,
        )

    def row_copy(d, s):
        return pltpu.make_async_remote_copy(
            src_ref=coeff_hbm.at[s, edge[d]],
            dst_ref=halo_coeff.at[d, s],
            send_sem=row_send.at[d, s],
            recv_sem=row_recv.at[d, s],
            device_id={"rows": target[d]},
            device_id_type=MESH,
        )

    first = (specs + 1) // 2
    for d in range(2):
        @pl.when(sends[d])
        def _():
            for a in range(2):
                box_copy(d, a).start()
            for s in range(first):
                row_copy(d, s).start()

    coeff_loads = [
        pltpu.make_async_copy(coeff_hbm.at[s], coeff.at[s], coeff_sem.at[s]) for s in range(specs)
    ]
    for copy in coeff_loads:
        copy.start()

    for d in range(2):
        @pl.when(jnp.logical_not(exists[d]))
        def _():
            halo_box[d] = jnp.zeros(halo_box.shape[1:], F32)

    zeros = jnp.zeros((chans, chans), F32)
    back = jnp.concatenate(
        [
            jnp.concatenate([weight_ref[2 - k, 2 - j] for k in range(3)] + [zeros], axis=1)
            for j in range(3)
        ],
        axis=0,
    )
    bias_row = bias_ref[...]
    bias_high = bias_row.astype(BF16).astype(F32)
    bias_mid = (bias_row - bias_high).astype(BF16).astype(F32)
    bias_low = bias_row - bias_high - bias_mid
    zrow = jnp.zeros((1, chans), F32)
    bias_parts = (bias_high, bias_mid, bias_low)

    def bias_rows(own):
        lines = [
            jnp.concatenate([part if k in own else zrow for k in range(4)], axis=1)
            for part in bias_parts
        ]
        return jnp.concatenate(lines + [jnp.zeros((13, 4 * chans), F32)], axis=0)

    back_weight[pl.ds(0, 6 * chans)] = jnp.concatenate(
        [back, pltpu.roll(back, chans, 1)], axis=0
    ).astype(BF16)
    back_weight[pl.ds(6 * chans, 16)] = bias_rows((1, 2)).astype(BF16)
    back_weight[pl.ds(6 * chans + 16, 16)] = bias_rows((1,)).astype(BF16)

    wide = jnp.concatenate(
        [
            jnp.concatenate([weight_ref[k, j] for j in range(3)] + [zeros], axis=1)
            for k in range(3)
        ]
        + [jnp.zeros((chans, 4 * chans), F32)],
        axis=0,
    )
    fore = wide.T[: 3 * chans]
    fore = jnp.concatenate([fore, pltpu.roll(fore, chans, 1)], axis=0)
    for ref, value in ((box_weight, fore), (rad_weight, jnp.abs(fore))):
        high, low = split2(value)
        ref[...] = jnp.concatenate([high, low, high], axis=1)

    eye = lax.broadcasted_iota(jnp.int32, (chans, chans), 0) == lax.broadcasted_iota(
        jnp.int32, (chans, chans), 1
    )
    bias_col[...] = jnp.broadcast_to(
        jnp.sum(jnp.where(eye, jnp.broadcast_to(bias_row, (chans, chans)), 0.0), axis=1, keepdims=True),
        (chans, 128),
    )

    where_in_table = (
        lax.broadcasted_iota(jnp.int32, table_ref.shape, 0) * 128
        + lax.broadcasted_iota(jnp.int32, table_ref.shape, 1)
    )
    for s in range(specs):
        table_vec[pl.ds(s, 1), :] = jnp.sum(
            jnp.where(where_in_table == ids_ref[s], table_ref[...], 0.0), axis=0, keepdims=True
        )
    acc[...] = jnp.zeros(acc.shape, F32)

    def field(four_rows, weight):
        high, low = split2(four_rows)
        return jnp.dot(
            weight, jnp.concatenate([high, high, low], axis=0), preferred_element_type=F32
        )

    def relax(h, c_res, r_res):
        blocks = [slice(j * chans, (j + 1) * chans) for j in range(3)]
        center_out = combine(*(c_res[b] for b in blocks)) + bias_col[:, :1]
        radius_out = combine(*(r_res[b] for b in blocks))
        upper = center_out + radius_out
        lower = center_out - radius_out
        spread = 2.0 * radius_out
        relaxed = jnp.minimum(jnp.maximum(upper, 0.0), spread) / spread
        state = status[h]
        slope = jnp.where(state == 2, relaxed, jnp.where(state == 1, 1.0, 0.0))
        slopes[h] = slope.astype(BF16)
        cut = jnp.where(state == 2, -relaxed * jnp.minimum(lower, 0.0), 0.0)
        icept[h] = cut.astype(BF16).astype(F32)
        low_end[h] = center[h + 1] - radius[h + 1]
        high_end[h] = center[h + 1] + radius[h + 1]

    for copy in loads:
        copy.wait()

    pairs = (rows - 2) // 2

    def inner_slopes(p, carry):
        h = 1 + 2 * p
        four = lambda ref: ref[pl.ds(h, 4)].reshape(4 * chans, cols)
        c_res = field(four(center), box_weight[...])
        r_res = field(four(radius), rad_weight[...])
        for r in range(2):
            block = slice(3 * chans * r, 3 * chans * (r + 1))
            relax(h + r, c_res[block], r_res[block])
        return carry

    lax.fori_loop(0, pairs, inner_slopes, 0)

    for d in range(2):
        @pl.when(exists[d])
        def _():
            for a in range(2):
                box_copy(d, a).wait_recv()
            pass_copy(d).start()
    for d in range(2):
        @pl.when(exists[d])
        def _():
            pass_copy(d).wait()

    blank = jnp.zeros((chans, cols), F32)
    for d, ref_row in ((0, 0), (1, rows - 1)):
        def three(a, ref):
            own = [ref[1], ref[2]] if d == 0 else [ref[rows - 1], ref[rows]]
            halo = [halo_box[d, a]]
            return jnp.concatenate((halo + own if d == 0 else own + halo) + [blank], axis=0)

        c_res = field(three(0, center), box_weight[pl.ds(0, 3 * chans)])
        r_res = field(three(1, radius), rad_weight[pl.ds(0, 3 * chans)])
        relax(ref_row, c_res, r_res)

    for d in range(2):
        @pl.when(sends[d])
        def _():
            slope_copy(d).start()
            for s in range(first, specs):
                row_copy(d, s).start()

    def finish(s, h, result):
        value = combine(*(result[j * chans : (j + 1) * chans] for j in range(3)))
        out_ref[s, h] = value.astype(BF16)
        return fold(jnp.minimum(value * low_end[h], value * high_end[h]))

    def offset(s, h):
        return fold(jnp.minimum(coeff[s, h], 0).astype(F32) * icept[h])

    def edge_row(s, d, halo):
        h = 0 if d == 0 else rows - 1
        own = pl.ds(0, 2) if d == 0 else pl.ds(rows - 2, 2)
        pre = (coeff[s, own] * slopes[own]).reshape(2 * chans, cols)
        stack = [halo, pre] if d == 0 else [pre, halo]
        four = jnp.concatenate(stack + [jnp.zeros((chans, cols), BF16)], axis=0)
        result = jnp.dot(back_weight[pl.ds(0, 3 * chans)], four, preferred_element_type=F32)
        extra = jnp.dot(
            back_weight[pl.ds(6 * chans + 16, 16)], four, preferred_element_type=F32
        )
        acc[s] += finish(s, h, result) + fold(extra)

    for copy in coeff_loads:
        copy.wait()

    def inner(s, carry):
        total = offset(s, 0) + offset(s, rows - 1)
        for p in range(pairs):
            h = 1 + 2 * p
            pre = (coeff[s, pl.ds(h - 1, 4)] * slopes[pl.ds(h - 1, 4)]).reshape(4 * chans, cols)
            result = jnp.dot(
                back_weight[pl.ds(0, 6 * chans + 16)], pre, preferred_element_type=F32
            )
            for r in range(2):
                total += finish(s, h + r, result[3 * chans * r : 3 * chans * (r + 1)])
                total += offset(s, h + r)
            total += fold(result[6 * chans :])
        acc[s] += total
        return carry

    lax.fori_loop(0, specs, inner, 0)

    for d in range(2):
        @pl.when(jnp.logical_not(exists[d]))
        def _():
            def at_border(s, carry):
                edge_row(s, d, jnp.zeros((chans, cols), BF16))
                return carry

            lax.fori_loop(0, specs, at_border, 0)

    for d in range(2):
        @pl.when(exists[d])
        def _():
            slope_copy(d).wait_recv()
            spass_copy(d).start()
    for d in range(2):
        @pl.when(exists[d])
        def _():
            spass_copy(d).wait()

            def at_halo(s, carry):
                row_copy(d, s).wait_recv()
                edge_row(s, d, halo_coeff[d, s] * edge_slopes[d])
                return carry

            lax.fori_loop(0, specs, at_halo, 0)

    folded = jnp.sum(acc[...], axis=1)
    share = folded[:, :128]
    for t in range(1, cols // 128):
        share += folded[:, 128 * t : 128 * (t + 1)]
    parts[0] = share

    def part_copy(step):
        return pltpu.make_async_remote_copy(
            src_ref=parts.at[0],
            dst_ref=parts.at[step],
            send_sem=part_send.at[step],
            recv_sem=part_recv.at[step],
            device_id={"rows": lax.rem(me + step, n_rows)},
            device_id_type=MESH,
        )

    for step in range(1, n_rows):
        part_copy(step).start()
    for d in range(2):
        @pl.when(sends[d])
        def _():
            for a in range(2):
                box_copy(d, a).wait_send()
            slope_copy(d).wait_send()
            for s in range(specs):
                row_copy(d, s).wait_send()
    for step in range(1, n_rows):
        part_copy(step).wait()
    total = parts[0]
    for step in range(1, n_rows):
        total += parts[step]
    bound = jnp.sum(
        total * (1.0 / (rows * n_rows * cols)) + table_vec[...], axis=1, keepdims=True
    )
    shape = (specs, 128)
    diagonal = lax.broadcasted_iota(jnp.int32, shape, 0) == lax.broadcasted_iota(
        jnp.int32, shape, 1
    )
    line = jnp.sum(jnp.where(diagonal, jnp.broadcast_to(bound, shape), 0.0), axis=0, keepdims=True)
    bounds_ref[...] = line[:, :specs]


def per_device(
    center, radius, conv_weight, conv_bias, split_status, out_coeffs, spec_ids, spec_offsets
):
    n_rows = lax.axis_size("rows")
    specs, rows, cols, chans = out_coeffs.shape
    swap3 = lambda x: jnp.transpose(x, (0, 2, 1))
    dma = pltpu.SemaphoreType.DMA
    vmem = pl.BlockSpec(memory_space=pltpu.VMEM)
    anywhere = pl.BlockSpec(memory_space=pl.ANY)
    out, bounds = pl.pallas_call(
        functools.partial(kernel, n_rows),
        out_shape=(
            jax.ShapeDtypeStruct((specs, rows, chans, cols), BF16),
            jax.ShapeDtypeStruct((1, specs), F32),
        ),
        in_specs=[
            anywhere, anywhere, vmem, vmem, anywhere, anywhere,
            pl.BlockSpec(memory_space=pltpu.SMEM), vmem,
        ],
        out_specs=(vmem, vmem),
        scratch_shapes=[
            pltpu.VMEM((rows + 2, chans, cols), F32),
            pltpu.VMEM((rows + 2, chans, cols), F32),
            pltpu.VMEM((rows, chans, cols), jnp.int32),
            pltpu.VMEM((specs, rows, chans, cols), BF16),
            pltpu.VMEM((rows, chans, cols), F32),
            pltpu.VMEM((rows, chans, cols), F32),
            pltpu.VMEM((rows, chans, cols), BF16),
            pltpu.VMEM((rows, chans, cols), F32),
            pltpu.VMEM((2, chans, cols), BF16),
            pltpu.VMEM((2, 2, chans, cols), F32),
            pltpu.VMEM((2, specs, chans, cols), BF16),
            pltpu.VMEM((6 * chans, 12 * chans), BF16),
            pltpu.VMEM((6 * chans, 12 * chans), BF16),
            pltpu.VMEM((6 * chans + 32, 4 * chans), BF16),
            pltpu.VMEM((chans, 128), F32),
            pltpu.VMEM((specs, 8, cols), F32),
            pltpu.VMEM((n_rows, specs, 128), F32),
            pltpu.VMEM((specs, 128), F32),
            dma((3,)), dma((specs,)),
            dma((2, 2)), dma((2, 2)), dma((2,)), dma((2,)),
            dma((2,)), dma((2,)), dma((2,)), dma((2,)),
            dma((2, specs)), dma((2, specs)), dma((n_rows,)), dma((n_rows,)),
        ],
        compiler_params=pltpu.CompilerParams(
            collective_id=0, has_side_effects=True, vmem_limit_bytes=48 * 1024 * 1024
        ),
        name="bound_pass",
    )(
        swap3(center),
        swap3(radius),
        conv_weight,
        conv_bias.reshape(1, chans),
        swap3(split_status),
        jnp.transpose(out_coeffs, (0, 1, 3, 2)),
        spec_ids,
        spec_offsets.reshape(-1, 128),
    )
    return jnp.transpose(out, (0, 1, 3, 2)), bounds.reshape(specs)


def solution(mesh):
    in_specs = (
        P("rows", None, None),
        P("rows", None, None),
        P(),
        P(),
        P("rows", None, None),
        P("specs", "rows", None, None),
        P("specs"),
        P(),
    )
    out_specs = (P("specs", "rows", None, None), P("specs"))
    return jax.shard_map(
        per_device, mesh=mesh, in_specs=in_specs, out_specs=out_specs, check_vma=False
    )
```

```python
import functools

import jax
import jax.numpy as jnp
from jax import lax
from jax.experimental import pallas as pl
from jax.experimental.pallas import tpu as pltpu
from jax.sharding import PartitionSpec as P

F32 = jnp.float32
BF16 = jnp.bfloat16
MESH = pl.DeviceIdType.MESH


def split2(value):
    high = value.astype(BF16)
    return high, (value - high.astype(F32)).astype(BF16)


def combine(first, middle, last):
    width = first.shape[1]
    rolled = pltpu.roll(first, 1, 1)
    lane = lax.broadcasted_iota(jnp.int32, (first.shape[0], 128), 1)
    rolled = jnp.concatenate(
        [jnp.where(lane == 0, 0.0, rolled[:, :128]), rolled[:, 128:]], axis=1
    )
    back = pltpu.roll(last, width - 1, 1)
    back = jnp.concatenate(
        [back[:, :-128], jnp.where(lane == 127, 0.0, back[:, -128:])], axis=1
    )
    return rolled + middle + back


def fold(value):
    rows, width = value.shape
    return jnp.sum(value.reshape(rows // 8, 8, width), axis=0)


def kernel(
    n_rows,
    center_hbm, radius_hbm, weight_hbm, bias_hbm, status_hbm, coeff_hbm, ids_hbm, table_hbm,
    out_ref, bounds_ref,
    center, radius, status, coeff, weight_ref, bias_ref, ids_ref, table_ref,
    low_end, high_end, slopes, icept, edge_slopes,
    halo_box, halo_coeff, box_weight, rad_weight, back_weight, bias_col,
    acc, parts, table_vec,
    load_sem, coeff_sem, box_send, box_recv, pass_send, pass_recv,
    slope_send, slope_recv, spass_send, spass_recv, row_send, row_recv, part_send, part_recv,
):
    specs, rows, chans, cols = coeff.shape
    half = chans // 2
    me = lax.axis_index("rows")
    lane_dev = lax.axis_index("specs")
    core = lax.rem(lane_dev, 2)
    partner = lane_dev + 1 - 2 * core
    has_prev = me > 0
    has_next = me < n_rows - 1
    mine = pl.ds(pl.multiple_of(core * half, half), half)
    exists = (has_prev, has_next)
    sends = (has_next, has_prev)
    target = (me + 1, me - 1)
    edge = (rows - 1, 0)

    loads = [
        pltpu.make_async_copy(center_hbm, center.at[pl.ds(1, rows)], load_sem.at[0]),
        pltpu.make_async_copy(radius_hbm, radius.at[pl.ds(1, rows)], load_sem.at[1]),
        pltpu.make_async_copy(status_hbm, status, load_sem.at[2]),
    ]
    small = [
        pltpu.make_async_copy(weight_hbm, weight_ref, load_sem.at[3]),
        pltpu.make_async_copy(bias_hbm, bias_ref, load_sem.at[4]),
        pltpu.make_async_copy(ids_hbm, ids_ref, load_sem.at[5]),
        pltpu.make_async_copy(table_hbm, table_ref, load_sem.at[6]),
    ]
    for copy in small + loads:
        copy.start()

    barrier = pltpu.get_barrier_semaphore()
    for step in range(1, n_rows):
        pl.semaphore_signal(
            barrier, inc=1, device_id={"rows": lax.rem(me + step, n_rows)}, device_id_type=MESH
        )
    pl.semaphore_signal(barrier, inc=1, device_id={"specs": partner}, device_id_type=MESH)
    pl.semaphore_wait(barrier, n_rows)

    def box_copy(d, a):
        return pltpu.make_async_remote_copy(
            src_ref=(center_hbm, radius_hbm)[a].at[edge[d], mine],
            dst_ref=halo_box.at[d, a, mine],
            send_sem=box_send.at[d, a],
            recv_sem=box_recv.at[d, a],
            device_id={"rows": target[d]},
            device_id_type=MESH,
        )

    def pass_copy(d):
        return pltpu.make_async_remote_copy(
            src_ref=halo_box.at[d, :, mine],
            dst_ref=halo_box.at[d, :, mine],
            send_sem=pass_send.at[d],
            recv_sem=pass_recv.at[d],
            device_id={"specs": partner},
            device_id_type=MESH,
        )

    def slope_copy(d):
        return pltpu.make_async_remote_copy(
            src_ref=slopes.at[edge[d], mine],
            dst_ref=edge_slopes.at[d, mine],
            send_sem=slope_send.at[d],
            recv_sem=slope_recv.at[d],
            device_id={"rows": target[d]},
            device_id_type=MESH,
        )

    def spass_copy(d):
        return pltpu.make_async_remote_copy(
            src_ref=edge_slopes.at[d, mine],
            dst_ref=edge_slopes.at[d, mine],
            send_sem=spass_send.at[d],
            recv_sem=spass_recv.at[d],
            device_id={"specs": partner},
            device_id_type=MESH,
        )

    def row_copy(d, s):
        return pltpu.make_async_remote_copy(
            src_ref=coeff_hbm.at[s, edge[d]],
            dst_ref=halo_coeff.at[d, s],
            send_sem=row_send.at[d, s],
            recv_sem=row_recv.at[d, s],
            device_id={"rows": target[d]},
            device_id_type=MESH,
        )

    first = (specs + 1) // 2
    for d in range(2):
        @pl.when(sends[d])
        def _():
            for a in range(2):
                box_copy(d, a).start()
            for s in range(first):
                row_copy(d, s).start()

    coeff_loads = [
        pltpu.make_async_copy(coeff_hbm.at[s], coeff.at[s], coeff_sem.at[s]) for s in range(specs)
    ]
    for copy in coeff_loads:
        copy.start()

    for d in range(2):
        @pl.when(jnp.logical_not(exists[d]))
        def _():
            halo_box[d] = jnp.zeros(halo_box.shape[1:], F32)

    for copy in small:
        copy.wait()

    zeros = jnp.zeros((chans, chans), F32)
    back = jnp.concatenate(
        [
            jnp.concatenate([weight_ref[2 - k, 2 - j] for k in range(3)] + [zeros], axis=1)
            for j in range(3)
        ],
        axis=0,
    )
    bias_row = bias_ref[...]
    bias_high = bias_row.astype(BF16).astype(F32)
    bias_mid = (bias_row - bias_high).astype(BF16).astype(F32)
    bias_low = bias_row - bias_high - bias_mid
    zrow = jnp.zeros((1, chans), F32)
    bias_parts = (bias_high, bias_mid, bias_low)

    def bias_rows(own):
        lines = [
            jnp.concatenate([part if k in own else zrow for k in range(4)], axis=1)
            for part in bias_parts
        ]
        return jnp.concatenate(lines + [jnp.zeros((13, 4 * chans), F32)], axis=0)

    back_weight[pl.ds(0, 6 * chans)] = jnp.concatenate(
        [back, pltpu.roll(back, chans, 1)], axis=0
    ).astype(BF16)
    back_weight[pl.ds(6 * chans, 16)] = bias_rows((1, 2)).astype(BF16)
    back_weight[pl.ds(6 * chans + 16, 16)] = bias_rows((1,)).astype(BF16)

    wide = jnp.concatenate(
        [
            jnp.concatenate([weight_ref[k, j] for j in range(3)] + [zeros], axis=1)
            for k in range(3)
        ]
        + [jnp.zeros((chans, 4 * chans), F32)],
        axis=0,
    )
    fore = wide.T[: 3 * chans]
    fore = jnp.concatenate([fore, pltpu.roll(fore, chans, 1)], axis=0)
    for ref, value in ((box_weight, fore), (rad_weight, jnp.abs(fore))):
        high, low = split2(value)
        ref[...] = jnp.concatenate([high, low, high], axis=1)

    eye = lax.broadcasted_iota(jnp.int32, (chans, chans), 0) == lax.broadcasted_iota(
        jnp.int32, (chans, chans), 1
    )
    bias_col[...] = jnp.broadcast_to(
        jnp.sum(jnp.where(eye, jnp.broadcast_to(bias_row, (chans, chans)), 0.0), axis=1, keepdims=True),
        (chans, 128),
    )

    where_in_table = (
        lax.broadcasted_iota(jnp.int32, table_ref.shape, 0) * 128
        + lax.broadcasted_iota(jnp.int32, table_ref.shape, 1)
    )
    for s in range(specs):
        table_vec[pl.ds(s, 1), :] = jnp.sum(
            jnp.where(where_in_table == ids_ref[s], table_ref[...], 0.0), axis=0, keepdims=True
        )
    acc[...] = jnp.zeros(acc.shape, F32)

    def field(four_rows, weight):
        high, low = split2(four_rows)
        return jnp.dot(
            weight, jnp.concatenate([high, high, low], axis=0), preferred_element_type=F32
        )

    def relax(h, c_res, r_res):
        blocks = [slice(j * chans, (j + 1) * chans) for j in range(3)]
        center_out = combine(*(c_res[b] for b in blocks)) + bias_col[:, :1]
        radius_out = combine(*(r_res[b] for b in blocks))
        upper = center_out + radius_out
        lower = center_out - radius_out
        spread = 2.0 * radius_out
        relaxed = jnp.minimum(jnp.maximum(upper, 0.0), spread) / spread
        state = status[h]
        slope = jnp.where(state == 2, relaxed, jnp.where(state == 1, 1.0, 0.0))
        slopes[h] = slope.astype(BF16)
        cut = jnp.where(state == 2, -relaxed * jnp.minimum(lower, 0.0), 0.0)
        icept[h] = cut.astype(BF16).astype(F32)
        low_end[h] = center[h + 1] - radius[h + 1]
        high_end[h] = center[h + 1] + radius[h + 1]

    for copy in loads:
        copy.wait()

    pairs = (rows - 2) // 2

    def inner_slopes(p, carry):
        h = 1 + 2 * p
        four = lambda ref: ref[pl.ds(h, 4)].reshape(4 * chans, cols)
        c_res = field(four(center), box_weight[...])
        r_res = field(four(radius), rad_weight[...])
        for r in range(2):
            block = slice(3 * chans * r, 3 * chans * (r + 1))
            relax(h + r, c_res[block], r_res[block])
        return carry

    lax.fori_loop(0, pairs, inner_slopes, 0)

    for d in range(2):
        @pl.when(exists[d])
        def _():
            for a in range(2):
                box_copy(d, a).wait_recv()
            pass_copy(d).start()
    for d in range(2):
        @pl.when(exists[d])
        def _():
            pass_copy(d).wait()

    blank = jnp.zeros((chans, cols), F32)
    for d, ref_row in ((0, 0), (1, rows - 1)):
        def three(a, ref):
            own = [ref[1], ref[2]] if d == 0 else [ref[rows - 1], ref[rows]]
            halo = [halo_box[d, a]]
            return jnp.concatenate((halo + own if d == 0 else own + halo) + [blank], axis=0)

        c_res = field(three(0, center), box_weight[pl.ds(0, 3 * chans)])
        r_res = field(three(1, radius), rad_weight[pl.ds(0, 3 * chans)])
        relax(ref_row, c_res, r_res)

    for d in range(2):
        @pl.when(sends[d])
        def _():
            slope_copy(d).start()
            for s in range(first, specs):
                row_copy(d, s).start()

    def finish(s, h, result):
        value = combine(*(result[j * chans : (j + 1) * chans] for j in range(3)))
        out_ref[s, h] = value.astype(BF16)
        return fold(jnp.minimum(value * low_end[h], value * high_end[h]))

    def offset(s, h):
        return fold(jnp.minimum(coeff[s, h], 0).astype(F32) * icept[h])

    def edge_row(s, d, halo):
        h = 0 if d == 0 else rows - 1
        own = pl.ds(0, 2) if d == 0 else pl.ds(rows - 2, 2)
        pre = (coeff[s, own] * slopes[own]).reshape(2 * chans, cols)
        stack = [halo, pre] if d == 0 else [pre, halo]
        four = jnp.concatenate(stack + [jnp.zeros((chans, cols), BF16)], axis=0)
        result = jnp.dot(back_weight[pl.ds(0, 3 * chans)], four, preferred_element_type=F32)
        extra = jnp.dot(
            back_weight[pl.ds(6 * chans + 16, 16)], four, preferred_element_type=F32
        )
        acc[s] += finish(s, h, result) + fold(extra)

    for copy in coeff_loads:
        copy.wait()

    def inner(s, carry):
        total = offset(s, 0) + offset(s, rows - 1)
        for p in range(pairs):
            h = 1 + 2 * p
            pre = (coeff[s, pl.ds(h - 1, 4)] * slopes[pl.ds(h - 1, 4)]).reshape(4 * chans, cols)
            result = jnp.dot(
                back_weight[pl.ds(0, 6 * chans + 16)], pre, preferred_element_type=F32
            )
            for r in range(2):
                total += finish(s, h + r, result[3 * chans * r : 3 * chans * (r + 1)])
                total += offset(s, h + r)
            total += fold(result[6 * chans :])
        acc[s] += total
        return carry

    lax.fori_loop(0, specs, inner, 0)

    for d in range(2):
        @pl.when(jnp.logical_not(exists[d]))
        def _():
            def at_border(s, carry):
                edge_row(s, d, jnp.zeros((chans, cols), BF16))
                return carry

            lax.fori_loop(0, specs, at_border, 0)

    for d in range(2):
        @pl.when(exists[d])
        def _():
            slope_copy(d).wait_recv()
            spass_copy(d).start()
    for d in range(2):
        @pl.when(exists[d])
        def _():
            spass_copy(d).wait()

            def at_halo(s, carry):
                row_copy(d, s).wait_recv()
                edge_row(s, d, halo_coeff[d, s] * edge_slopes[d])
                return carry

            lax.fori_loop(0, specs, at_halo, 0)

    folded = jnp.sum(acc[...], axis=1)
    share = folded[:, :128]
    for t in range(1, cols // 128):
        share += folded[:, 128 * t : 128 * (t + 1)]
    parts[0] = share

    def part_copy(step):
        return pltpu.make_async_remote_copy(
            src_ref=parts.at[0],
            dst_ref=parts.at[step],
            send_sem=part_send.at[step],
            recv_sem=part_recv.at[step],
            device_id={"rows": lax.rem(me + step, n_rows)},
            device_id_type=MESH,
        )

    for step in range(1, n_rows):
        part_copy(step).start()
    for d in range(2):
        @pl.when(sends[d])
        def _():
            for a in range(2):
                box_copy(d, a).wait_send()
            slope_copy(d).wait_send()
            for s in range(specs):
                row_copy(d, s).wait_send()
    for step in range(1, n_rows):
        part_copy(step).wait()
    total = parts[0]
    for step in range(1, n_rows):
        total += parts[step]
    bound = jnp.sum(
        total * (1.0 / (rows * n_rows * cols)) + table_vec[...], axis=1, keepdims=True
    )
    shape = (specs, 128)
    diagonal = lax.broadcasted_iota(jnp.int32, shape, 0) == lax.broadcasted_iota(
        jnp.int32, shape, 1
    )
    line = jnp.sum(jnp.where(diagonal, jnp.broadcast_to(bound, shape), 0.0), axis=0, keepdims=True)
    bounds_ref[...] = line[:, :specs]


def store_kernel(out_vmem, bounds_vmem, out_hbm, bounds_hbm, sem):
    specs = out_vmem.shape[0]
    copies = [
        pltpu.make_async_copy(out_vmem.at[s], out_hbm.at[s], sem.at[s]) for s in range(specs)
    ]
    copies.append(pltpu.make_async_copy(bounds_vmem, bounds_hbm, sem.at[specs]))
    for copy in copies:
        copy.start()
    for copy in copies:
        copy.wait()


def per_device(
    center, radius, conv_weight, conv_bias, split_status, out_coeffs, spec_ids, spec_offsets
):
    n_rows = lax.axis_size("rows")
    specs, rows, cols, chans = out_coeffs.shape
    swap3 = lambda x: jnp.transpose(x, (0, 2, 1))
    dma = pltpu.SemaphoreType.DMA
    vmem = pl.BlockSpec(memory_space=pltpu.VMEM)
    out, bounds = pl.pallas_call(
        functools.partial(kernel, n_rows),
        out_shape=(
            pltpu.VMEM((specs, rows, chans, cols), BF16),
            pltpu.VMEM((1, specs), F32),
        ),
        in_specs=[
            pl.BlockSpec(memory_space=pltpu.HBM),
        ] * 8,
        out_specs=(vmem, vmem),
        scratch_shapes=[
            pltpu.VMEM((rows + 2, chans, cols), F32),
            pltpu.VMEM((rows + 2, chans, cols), F32),
            pltpu.VMEM((rows, chans, cols), jnp.int32),
            pltpu.VMEM((specs, rows, chans, cols), BF16),
            pltpu.VMEM(conv_weight.shape, F32),
            pltpu.VMEM((1, chans), F32),
            pltpu.SMEM((specs,), jnp.int32),
            pltpu.VMEM((spec_offsets.shape[0] // 128, 128), F32),
            pltpu.VMEM((rows, chans, cols), F32),
            pltpu.VMEM((rows, chans, cols), F32),
            pltpu.VMEM((rows, chans, cols), BF16),
            pltpu.VMEM((rows, chans, cols), F32),
            pltpu.VMEM((2, chans, cols), BF16),
            pltpu.VMEM((2, 2, chans, cols), F32),
            pltpu.VMEM((2, specs, chans, cols), BF16),
            pltpu.VMEM((6 * chans, 12 * chans), BF16),
            pltpu.VMEM((6 * chans, 12 * chans), BF16),
            pltpu.VMEM((6 * chans + 32, 4 * chans), BF16),
            pltpu.VMEM((chans, 128), F32),
            pltpu.VMEM((specs, 8, cols), F32),
            pltpu.VMEM((n_rows, specs, 128), F32),
            pltpu.VMEM((specs, 128), F32),
            dma((7,)), dma((specs,)),
            dma((2, 2)), dma((2, 2)), dma((2,)), dma((2,)),
            dma((2,)), dma((2,)), dma((2,)), dma((2,)),
            dma((2, specs)), dma((2, specs)), dma((n_rows,)), dma((n_rows,)),
        ],
        compiler_params=pltpu.CompilerParams(
            collective_id=0, has_side_effects=True, vmem_limit_bytes=48 * 1024 * 1024
        ),
        name="bound_pass",
    )(
        *(
            pltpu.with_memory_space_constraint(x, pltpu.HBM)
            for x in (
                swap3(center),
                swap3(radius),
                conv_weight,
                conv_bias.reshape(1, chans),
                swap3(split_status),
                jnp.transpose(out_coeffs, (0, 1, 3, 2)),
                spec_ids,
                spec_offsets.reshape(-1, 128),
            )
        )
    )
    hbm = pl.BlockSpec(memory_space=pltpu.HBM)
    out, bounds = pl.pallas_call(
        store_kernel,
        out_shape=(
            jax.ShapeDtypeStruct((specs, rows, chans, cols), BF16),
            jax.ShapeDtypeStruct((1, specs), F32),
        ),
        in_specs=[vmem, vmem],
        out_specs=(hbm, hbm),
        scratch_shapes=[dma((specs + 1,))],
        name="store",
    )(out, bounds)
    return jnp.transpose(out, (0, 1, 3, 2)), bounds.reshape(specs)


def solution(mesh):
    in_specs = (
        P("rows", None, None),
        P("rows", None, None),
        P(),
        P(),
        P("rows", None, None),
        P("specs", "rows", None, None),
        P("specs"),
        P(),
    )
    out_specs = (P("specs", "rows", None, None), P("specs"))
    return jax.shard_map(
        per_device, mesh=mesh, in_specs=in_specs, out_specs=out_specs, check_vma=False
    )
```

```python
import functools

import jax
import jax.numpy as jnp
from jax import lax
from jax.experimental import pallas as pl
from jax.experimental.pallas import tpu as pltpu
from jax.sharding import PartitionSpec as P

F32 = jnp.float32
BF16 = jnp.bfloat16
MESH = pl.DeviceIdType.MESH


def split2(value):
    high = value.astype(BF16)
    return high, (value - high.astype(F32)).astype(BF16)


def combine(first, middle, last):
    width = first.shape[1]
    rolled = pltpu.roll(first, 1, 1)
    lane = lax.broadcasted_iota(jnp.int32, (first.shape[0], 128), 1)
    rolled = jnp.concatenate(
        [jnp.where(lane == 0, 0.0, rolled[:, :128]), rolled[:, 128:]], axis=1
    )
    back = pltpu.roll(last, width - 1, 1)
    back = jnp.concatenate(
        [back[:, :-128], jnp.where(lane == 127, 0.0, back[:, -128:])], axis=1
    )
    return rolled + middle + back


def fold(value):
    rows, width = value.shape
    return jnp.sum(value.reshape(rows // 8, 8, width), axis=0)


def kernel(
    n_rows,
    center_hbm, radius_hbm, weight_hbm, bias_hbm, status_hbm, coeff_hbm, ids_hbm, table_hbm,
    out_ref, bounds_ref,
    center, radius, status, coeff, weight_ref, bias_ref, ids_ref, table_ref,
    low_end, high_end, slopes, icept, edge_slopes,
    halo_box, halo_coeff, shifted, box_weight, rad_weight, back_weight, edge_weight, bias_col,
    acc, parts, table_vec,
    load_sem, coeff_sem, box_send, box_recv, pass_send, pass_recv,
    slope_send, slope_recv, spass_send, spass_recv, row_send, row_recv, part_send, part_recv,
):
    specs, rows, chans, cols = coeff.shape
    half = chans // 2
    me = lax.axis_index("rows")
    lane_dev = lax.axis_index("specs")
    core = lax.rem(lane_dev, 2)
    partner = lane_dev + 1 - 2 * core
    has_prev = me > 0
    has_next = me < n_rows - 1
    mine = pl.ds(pl.multiple_of(core * half, half), half)
    exists = (has_prev, has_next)
    sends = (has_next, has_prev)
    target = (me + 1, me - 1)
    edge = (rows - 1, 0)

    loads = [
        pltpu.make_async_copy(center_hbm, center.at[pl.ds(1, rows)], load_sem.at[0]),
        pltpu.make_async_copy(radius_hbm, radius.at[pl.ds(1, rows)], load_sem.at[1]),
        pltpu.make_async_copy(status_hbm, status, load_sem.at[2]),
    ]
    small = [
        pltpu.make_async_copy(weight_hbm, weight_ref, load_sem.at[3]),
        pltpu.make_async_copy(bias_hbm, bias_ref, load_sem.at[4]),
        pltpu.make_async_copy(ids_hbm, ids_ref, load_sem.at[5]),
        pltpu.make_async_copy(table_hbm, table_ref, load_sem.at[6]),
    ]
    for copy in small + loads:
        copy.start()

    barrier = pltpu.get_barrier_semaphore()
    for step in range(1, n_rows):
        pl.semaphore_signal(
            barrier, inc=1, device_id={"rows": lax.rem(me + step, n_rows)}, device_id_type=MESH
        )
    pl.semaphore_signal(barrier, inc=1, device_id={"specs": partner}, device_id_type=MESH)
    pl.semaphore_wait(barrier, n_rows)

    def box_copy(d, a):
        return pltpu.make_async_remote_copy(
            src_ref=(center_hbm, radius_hbm)[a].at[edge[d], mine],
            dst_ref=halo_box.at[d, a, mine],
            send_sem=box_send.at[d, a],
            recv_sem=box_recv.at[d, a],
            device_id={"rows": target[d]},
            device_id_type=MESH,
        )

    def pass_copy(d):
        return pltpu.make_async_remote_copy(
            src_ref=halo_box.at[d, :, mine],
            dst_ref=halo_box.at[d, :, mine],
            send_sem=pass_send.at[d],
            recv_sem=pass_recv.at[d],
            device_id={"specs": partner},
            device_id_type=MESH,
        )

    def slope_copy(d):
        return pltpu.make_async_remote_copy(
            src_ref=slopes.at[edge[d], mine],
            dst_ref=edge_slopes.at[d, mine],
            send_sem=slope_send.at[d],
            recv_sem=slope_recv.at[d],
            device_id={"rows": target[d]},
            device_id_type=MESH,
        )

    def spass_copy(d):
        return pltpu.make_async_remote_copy(
            src_ref=edge_slopes.at[d, mine],
            dst_ref=edge_slopes.at[d, mine],
            send_sem=spass_send.at[d],
            recv_sem=spass_recv.at[d],
            device_id={"specs": partner},
            device_id_type=MESH,
        )

    def row_copy(d, s):
        return pltpu.make_async_remote_copy(
            src_ref=coeff_hbm.at[s, edge[d]],
            dst_ref=halo_coeff.at[d, s],
            send_sem=row_send.at[d, s],
            recv_sem=row_recv.at[d, s],
            device_id={"rows": target[d]},
            device_id_type=MESH,
        )

    first = (specs + 1) // 2
    for d in range(2):
        @pl.when(sends[d])
        def _():
            for a in range(2):
                box_copy(d, a).start()
            for s in range(first):
                row_copy(d, s).start()

    coeff_loads = [
        pltpu.make_async_copy(coeff_hbm.at[s], coeff.at[s], coeff_sem.at[s]) for s in range(specs)
    ]
    for copy in coeff_loads:
        copy.start()

    for d in range(2):
        @pl.when(jnp.logical_not(exists[d]))
        def _():
            halo_box[d] = jnp.zeros(halo_box.shape[1:], F32)

    for copy in small:
        copy.wait()

    zeros = jnp.zeros((chans, chans), F32)
    back = jnp.concatenate([weight_ref[2 - k, j] for k in range(3) for j in range(3)], axis=1)
    blank3 = jnp.zeros((chans, 3 * chans), F32)
    upper_rows = jnp.concatenate([back, blank3], axis=1).astype(BF16)
    lower_rows = jnp.concatenate([blank3, back], axis=1).astype(BF16)
    bias_row = bias_ref[...]
    bias_high = bias_row.astype(BF16).astype(F32)
    bias_mid = (bias_row - bias_high).astype(BF16).astype(F32)
    bias_low = bias_row - bias_high - bias_mid
    zrow = jnp.zeros((1, chans), F32)
    bias_parts = (bias_high, bias_mid, bias_low)

    def bias_rows(own):
        lines = [
            jnp.concatenate(
                [part if k in own and j == 1 else zrow for k in range(4) for j in range(3)], axis=1
            )
            for part in bias_parts
        ]
        return jnp.concatenate(lines + [jnp.zeros((13, 12 * chans), F32)], axis=0).astype(BF16)

    back_weight[...] = jnp.concatenate([upper_rows, lower_rows, bias_rows((1, 2))], axis=0)
    edge_weight[0] = jnp.concatenate([upper_rows, bias_rows((1,))], axis=0)
    edge_weight[1] = jnp.concatenate([lower_rows, bias_rows((2,))], axis=0)

    wide = jnp.concatenate(
        [
            jnp.concatenate([weight_ref[k, j] for j in range(3)] + [zeros], axis=1)
            for k in range(3)
        ]
        + [jnp.zeros((chans, 4 * chans), F32)],
        axis=0,
    )
    fore = wide.T[: 3 * chans]
    fore = jnp.concatenate([fore, pltpu.roll(fore, chans, 1)], axis=0)
    for ref, value in ((box_weight, fore), (rad_weight, jnp.abs(fore))):
        high, low = split2(value)
        ref[...] = jnp.concatenate([high, low, high], axis=1)

    eye = lax.broadcasted_iota(jnp.int32, (chans, chans), 0) == lax.broadcasted_iota(
        jnp.int32, (chans, chans), 1
    )
    bias_col[...] = jnp.broadcast_to(
        jnp.sum(jnp.where(eye, jnp.broadcast_to(bias_row, (chans, chans)), 0.0), axis=1, keepdims=True),
        (chans, 128),
    )

    where_in_table = (
        lax.broadcasted_iota(jnp.int32, table_ref.shape, 0) * 128
        + lax.broadcasted_iota(jnp.int32, table_ref.shape, 1)
    )
    for s in range(specs):
        table_vec[pl.ds(s, 1), :] = jnp.sum(
            jnp.where(where_in_table == ids_ref[s], table_ref[...], 0.0), axis=0, keepdims=True
        )

    def field(four_rows, weight):
        high, low = split2(four_rows)
        return jnp.dot(
            weight, jnp.concatenate([high, high, low], axis=0), preferred_element_type=F32
        )

    def relax(h, c_res, r_res):
        blocks = [slice(j * chans, (j + 1) * chans) for j in range(3)]
        center_out = combine(*(c_res[b] for b in blocks)) + bias_col[:, :1]
        radius_out = combine(*(r_res[b] for b in blocks))
        upper = center_out + radius_out
        lower = center_out - radius_out
        spread = 2.0 * radius_out
        relaxed = jnp.minimum(jnp.maximum(upper, 0.0), spread) / spread
        state = status[h]
        slope = jnp.where(state == 2, relaxed, jnp.where(state == 1, 1.0, 0.0))
        slopes[h] = slope.astype(BF16)
        cut = jnp.where(state == 2, -relaxed * jnp.minimum(lower, 0.0), 0.0)
        icept[h] = cut.astype(BF16).astype(F32)
        low_end[h] = center[h + 1] - radius[h + 1]
        high_end[h] = center[h + 1] + radius[h + 1]

    for copy in loads:
        copy.wait()

    pairs = (rows - 2) // 2

    def inner_slopes(p, carry):
        h = 1 + 2 * p
        four = lambda ref: ref[pl.ds(h, 4)].reshape(4 * chans, cols)
        c_res = field(four(center), box_weight[...])
        r_res = field(four(radius), rad_weight[...])
        for r in range(2):
            block = slice(3 * chans * r, 3 * chans * (r + 1))
            relax(h + r, c_res[block], r_res[block])
        return carry

    lax.fori_loop(0, pairs, inner_slopes, 0)

    for d in range(2):
        @pl.when(exists[d])
        def _():
            for a in range(2):
                box_copy(d, a).wait_recv()
            pass_copy(d).start()
    for d in range(2):
        @pl.when(exists[d])
        def _():
            pass_copy(d).wait()

    blank = jnp.zeros((chans, cols), F32)
    for d, ref_row in ((0, 0), (1, rows - 1)):
        def three(a, ref):
            own = [ref[1], ref[2]] if d == 0 else [ref[rows - 1], ref[rows]]
            halo = [halo_box[d, a]]
            return jnp.concatenate((halo + own if d == 0 else own + halo) + [blank], axis=0)

        c_res = field(three(0, center), box_weight[pl.ds(0, 3 * chans)])
        r_res = field(three(1, radius), rad_weight[pl.ds(0, 3 * chans)])
        relax(ref_row, c_res, r_res)

    for d in range(2):
        @pl.when(sends[d])
        def _():
            slope_copy(d).start()
            for s in range(first, specs):
                row_copy(d, s).start()

    def finish(s, h, value):
        out_ref[s, h] = value.astype(BF16)
        return fold(jnp.minimum(value * low_end[h], value * high_end[h]))

    lane = lax.broadcasted_iota(jnp.int32, (chans, 128), 1)

    def shifts(pre):
        none = jnp.zeros((chans, 128), BF16)
        ahead = pltpu.roll(pre, cols - 1, 1)
        ahead = jnp.concatenate(
            [ahead[:, :-128], jnp.where(lane == 127, none, ahead[:, -128:])], axis=1
        )
        behind = pltpu.roll(pre, 1, 1)
        behind = jnp.concatenate(
            [jnp.where(lane == 0, none, behind[:, :128]), behind[:, 128:]], axis=1
        )
        return ahead, pre, behind

    def edge_row(s, d, halo):
        h = 0 if d == 0 else rows - 1
        own = pl.ds(0, 3) if d == 0 else pl.ds(rows - 3, 3)
        near = shifted[s, own].reshape(9 * chans, cols)
        four = jnp.concatenate([*halo, near] if d == 0 else [near, *halo], axis=0)
        result = jnp.dot(edge_weight[d], four, preferred_element_type=F32)
        acc[s] += finish(s, h, result[:chans]) + fold(result[chans:])

    for copy in coeff_loads:
        copy.wait()

    def inner(s, carry):
        total = jnp.zeros((8, cols), F32)
        for h in range(rows):
            block = coeff[s, h]
            for j, moved in enumerate(shifts(block * slopes[h])):
                shifted[s, h, j] = moved
            total += fold(jnp.minimum(block, 0).astype(F32) * icept[h])
        for p in range(pairs):
            h = 1 + 2 * p
            pre = shifted[s, pl.ds(h - 1, 4)].reshape(12 * chans, cols)
            result = jnp.dot(back_weight[...], pre, preferred_element_type=F32)
            for r in range(2):
                total += finish(s, h + r, result[chans * r : chans * (r + 1)])
            total += fold(result[2 * chans :])
        acc[s] = total
        return carry

    lax.fori_loop(0, specs, inner, 0)

    for d in range(2):
        @pl.when(jnp.logical_not(exists[d]))
        def _():
            def at_border(s, carry):
                edge_row(s, d, [jnp.zeros((3 * chans, cols), BF16)])
                return carry

            lax.fori_loop(0, specs, at_border, 0)

    for d in range(2):
        @pl.when(exists[d])
        def _():
            slope_copy(d).wait_recv()
            spass_copy(d).start()
    for d in range(2):
        @pl.when(exists[d])
        def _():
            spass_copy(d).wait()

            def at_halo(s, carry):
                row_copy(d, s).wait_recv()
                edge_row(s, d, shifts(halo_coeff[d, s] * edge_slopes[d]))
                return carry

            lax.fori_loop(0, specs, at_halo, 0)

    folded = jnp.sum(acc[...], axis=1)
    share = folded[:, :128]
    for t in range(1, cols // 128):
        share += folded[:, 128 * t : 128 * (t + 1)]
    parts[0] = share

    def part_copy(step):
        return pltpu.make_async_remote_copy(
            src_ref=parts.at[0],
            dst_ref=parts.at[step],
            send_sem=part_send.at[step],
            recv_sem=part_recv.at[step],
            device_id={"rows": lax.rem(me + step, n_rows)},
            device_id_type=MESH,
        )

    for step in range(1, n_rows):
        part_copy(step).start()
    for d in range(2):
        @pl.when(sends[d])
        def _():
            for a in range(2):
                box_copy(d, a).wait_send()
            slope_copy(d).wait_send()
            for s in range(specs):
                row_copy(d, s).wait_send()
    for step in range(1, n_rows):
        part_copy(step).wait()
    total = parts[0]
    for step in range(1, n_rows):
        total += parts[step]
    bound = jnp.sum(
        total * (1.0 / (rows * n_rows * cols)) + table_vec[...], axis=1, keepdims=True
    )
    shape = (specs, 128)
    diagonal = lax.broadcasted_iota(jnp.int32, shape, 0) == lax.broadcasted_iota(
        jnp.int32, shape, 1
    )
    line = jnp.sum(jnp.where(diagonal, jnp.broadcast_to(bound, shape), 0.0), axis=0, keepdims=True)
    bounds_ref[...] = line[:, :specs]


def store_kernel(out_vmem, bounds_vmem, out_hbm, bounds_hbm, sem):
    specs = out_vmem.shape[0]
    copies = [
        pltpu.make_async_copy(out_vmem.at[s], out_hbm.at[s], sem.at[s]) for s in range(specs)
    ]
    copies.append(pltpu.make_async_copy(bounds_vmem, bounds_hbm, sem.at[specs]))
    for copy in copies:
        copy.start()
    for copy in copies:
        copy.wait()


def per_device(
    center, radius, conv_weight, conv_bias, split_status, out_coeffs, spec_ids, spec_offsets
):
    n_rows = lax.axis_size("rows")
    specs, rows, cols, chans = out_coeffs.shape
    swap3 = lambda x: jnp.transpose(x, (0, 2, 1))
    dma = pltpu.SemaphoreType.DMA
    vmem = pl.BlockSpec(memory_space=pltpu.VMEM)
    out, bounds = pl.pallas_call(
        functools.partial(kernel, n_rows),
        out_shape=(
            pltpu.VMEM((specs, rows, chans, cols), BF16),
            pltpu.VMEM((1, specs), F32),
        ),
        in_specs=[
            pl.BlockSpec(memory_space=pltpu.HBM),
        ] * 8,
        out_specs=(vmem, vmem),
        scratch_shapes=[
            pltpu.VMEM((rows + 2, chans, cols), F32),
            pltpu.VMEM((rows + 2, chans, cols), F32),
            pltpu.VMEM((rows, chans, cols), jnp.int32),
            pltpu.VMEM((specs, rows, chans, cols), BF16),
            pltpu.VMEM(conv_weight.shape, F32),
            pltpu.VMEM((1, chans), F32),
            pltpu.SMEM((specs,), jnp.int32),
            pltpu.VMEM((spec_offsets.shape[0] // 128, 128), F32),
            pltpu.VMEM((rows, chans, cols), F32),
            pltpu.VMEM((rows, chans, cols), F32),
            pltpu.VMEM((rows, chans, cols), BF16),
            pltpu.VMEM((rows, chans, cols), F32),
            pltpu.VMEM((2, chans, cols), BF16),
            pltpu.VMEM((2, 2, chans, cols), F32),
            pltpu.VMEM((2, specs, chans, cols), BF16),
            pltpu.VMEM((specs, rows, 3, chans, cols), BF16),
            pltpu.VMEM((6 * chans, 12 * chans), BF16),
            pltpu.VMEM((6 * chans, 12 * chans), BF16),
            pltpu.VMEM((2 * chans + 16, 12 * chans), BF16),
            pltpu.VMEM((2, chans + 16, 12 * chans), BF16),
            pltpu.VMEM((chans, 128), F32),
            pltpu.VMEM((specs, 8, cols), F32),
            pltpu.VMEM((n_rows, specs, 128), F32),
            pltpu.VMEM((specs, 128), F32),
            dma((7,)), dma((specs,)),
            dma((2, 2)), dma((2, 2)), dma((2,)), dma((2,)),
            dma((2,)), dma((2,)), dma((2,)), dma((2,)),
            dma((2, specs)), dma((2, specs)), dma((n_rows,)), dma((n_rows,)),
        ],
        compiler_params=pltpu.CompilerParams(
            collective_id=0, has_side_effects=True, vmem_limit_bytes=48 * 1024 * 1024
        ),
        name="bound_pass",
    )(
        *(
            pltpu.with_memory_space_constraint(x, pltpu.HBM)
            for x in (
                swap3(center),
                swap3(radius),
                conv_weight,
                conv_bias.reshape(1, chans),
                swap3(split_status),
                jnp.transpose(out_coeffs, (0, 1, 3, 2)),
                spec_ids,
                spec_offsets.reshape(-1, 128),
            )
        )
    )
    hbm = pl.BlockSpec(memory_space=pltpu.HBM)
    out, bounds = pl.pallas_call(
        store_kernel,
        out_shape=(
            jax.ShapeDtypeStruct((specs, rows, chans, cols), BF16),
            jax.ShapeDtypeStruct((1, specs), F32),
        ),
        in_specs=[vmem, vmem],
        out_specs=(hbm, hbm),
        scratch_shapes=[dma((specs + 1,))],
        compiler_params=pltpu.CompilerParams(vmem_limit_bytes=1024 * 1024),
        name="store",
    )(*(pltpu.with_memory_space_constraint(x, pltpu.VMEM) for x in (out, bounds)))
    return jnp.transpose(out, (0, 1, 3, 2)), bounds.reshape(specs)


def solution(mesh):
    in_specs = (
        P("rows", None, None),
        P("rows", None, None),
        P(),
        P(),
        P("rows", None, None),
        P("specs", "rows", None, None),
        P("specs"),
        P(),
    )
    out_specs = (P("specs", "rows", None, None), P("specs"))
    return jax.shard_map(
        per_device, mesh=mesh, in_specs=in_specs, out_specs=out_specs, check_vma=False
    )
```

```python
import functools

import jax
import jax.numpy as jnp
from jax import lax
from jax.experimental import pallas as pl
from jax.experimental.pallas import tpu as pltpu
from jax.sharding import PartitionSpec as P

F32 = jnp.float32
BF16 = jnp.bfloat16
MESH = pl.DeviceIdType.MESH


def split2(value):
    high = value.astype(BF16)
    return high, (value - high.astype(F32)).astype(BF16)


def combine(first, middle, last):
    width = first.shape[1]
    rolled = pltpu.roll(first, 1, 1)
    lane = lax.broadcasted_iota(jnp.int32, (first.shape[0], 128), 1)
    rolled = jnp.concatenate(
        [jnp.where(lane == 0, 0.0, rolled[:, :128]), rolled[:, 128:]], axis=1
    )
    back = pltpu.roll(last, width - 1, 1)
    back = jnp.concatenate(
        [back[:, :-128], jnp.where(lane == 127, 0.0, back[:, -128:])], axis=1
    )
    return rolled + middle + back


def fold(value):
    rows, width = value.shape
    return jnp.sum(value.reshape(rows // 8, 8, width), axis=0)


def kernel(
    n_rows,
    center_hbm, radius_hbm, weight_hbm, bias_hbm, status_hbm, coeff_hbm, ids_hbm, table_hbm,
    out_ref, bounds_ref,
    center, radius, status, coeff, weight_ref, bias_ref, ids_ref, table_ref,
    low_end, high_end, slopes, icept, edge_slopes,
    box_edge, halo_box, halo_coeff, shifted, box_weight, rad_weight, back_weight, edge_weight, bias_col,
    acc, parts, table_vec,
    load_sem, coeff_sem, box_send, box_recv, pass_send, pass_recv,
    slope_send, slope_recv, spass_send, spass_recv, row_send, row_recv, part_send, part_recv,
):
    specs, rows, chans, cols = coeff.shape
    half = chans // 2
    me = lax.axis_index("rows")
    lane_dev = lax.axis_index("specs")
    core = lax.rem(lane_dev, 2)
    partner = lane_dev + 1 - 2 * core
    has_prev = me > 0
    has_next = me < n_rows - 1
    mine = pl.ds(pl.multiple_of(core * half, half), half)
    exists = (has_prev, has_next)
    sends = (has_next, has_prev)
    target = (me + 1, me - 1)
    edge = (rows - 1, 0)

    loads = [
        pltpu.make_async_copy(center_hbm, center.at[pl.ds(1, rows)], load_sem.at[0]),
        pltpu.make_async_copy(radius_hbm, radius.at[pl.ds(1, rows)], load_sem.at[1]),
        pltpu.make_async_copy(status_hbm, status, load_sem.at[2]),
    ]
    small = [
        pltpu.make_async_copy(weight_hbm, weight_ref, load_sem.at[3]),
        pltpu.make_async_copy(bias_hbm, bias_ref, load_sem.at[4]),
        pltpu.make_async_copy(ids_hbm, ids_ref, load_sem.at[5]),
        pltpu.make_async_copy(table_hbm, table_ref, load_sem.at[6]),
    ]
    for copy in loads[:2] + small + loads[2:]:
        copy.start()

    barrier = pltpu.get_barrier_semaphore()
    for step in range(1, n_rows):
        pl.semaphore_signal(
            barrier, inc=1, device_id={"rows": lax.rem(me + step, n_rows)}, device_id_type=MESH
        )
    pl.semaphore_signal(barrier, inc=1, device_id={"specs": partner}, device_id_type=MESH)

    for copy in loads[:2]:
        copy.wait()
    for d in range(2):
        for a, ref in enumerate((center, radius)):
            box_edge[d, a] = ref[1 + edge[d]].astype(BF16)
    pl.semaphore_wait(barrier, n_rows)

    def box_copy(d):
        return pltpu.make_async_remote_copy(
            src_ref=box_edge.at[d, :, mine],
            dst_ref=halo_box.at[d, :, mine],
            send_sem=box_send.at[d],
            recv_sem=box_recv.at[d],
            device_id={"rows": target[d]},
            device_id_type=MESH,
        )

    def pass_copy(d):
        return pltpu.make_async_remote_copy(
            src_ref=halo_box.at[d, :, mine],
            dst_ref=halo_box.at[d, :, mine],
            send_sem=pass_send.at[d],
            recv_sem=pass_recv.at[d],
            device_id={"specs": partner},
            device_id_type=MESH,
        )

    def slope_copy(d):
        return pltpu.make_async_remote_copy(
            src_ref=slopes.at[edge[d], mine],
            dst_ref=edge_slopes.at[d, mine],
            send_sem=slope_send.at[d],
            recv_sem=slope_recv.at[d],
            device_id={"rows": target[d]},
            device_id_type=MESH,
        )

    def spass_copy(d):
        return pltpu.make_async_remote_copy(
            src_ref=edge_slopes.at[d, mine],
            dst_ref=edge_slopes.at[d, mine],
            send_sem=spass_send.at[d],
            recv_sem=spass_recv.at[d],
            device_id={"specs": partner},
            device_id_type=MESH,
        )

    def row_copy(d, s):
        return pltpu.make_async_remote_copy(
            src_ref=coeff_hbm.at[s, edge[d]],
            dst_ref=halo_coeff.at[d, s],
            send_sem=row_send.at[d, s],
            recv_sem=row_recv.at[d, s],
            device_id={"rows": target[d]},
            device_id_type=MESH,
        )

    first = specs // 2
    for d in range(2):
        @pl.when(sends[d])
        def _():
            box_copy(d).start()

    coeff_loads = [
        pltpu.make_async_copy(coeff_hbm.at[s], coeff.at[s], coeff_sem.at[s]) for s in range(specs)
    ]
    for copy in coeff_loads:
        copy.start()

    for d in range(2):
        @pl.when(jnp.logical_not(exists[d]))
        def _():
            halo_box[d] = jnp.zeros(halo_box.shape[1:], BF16)

    for copy in small:
        copy.wait()

    zeros = jnp.zeros((chans, chans), F32)
    back = jnp.concatenate([weight_ref[2 - k, j] for k in range(3) for j in range(3)], axis=1)
    blank3 = jnp.zeros((chans, 3 * chans), F32)
    upper_rows = jnp.concatenate([back, blank3], axis=1).astype(BF16)
    lower_rows = jnp.concatenate([blank3, back], axis=1).astype(BF16)
    bias_row = bias_ref[...]
    bias_high = bias_row.astype(BF16).astype(F32)
    bias_mid = (bias_row - bias_high).astype(BF16).astype(F32)
    bias_low = bias_row - bias_high - bias_mid
    zrow = jnp.zeros((1, chans), F32)
    bias_parts = (bias_high, bias_mid, bias_low)

    def bias_rows(own):
        lines = [
            jnp.concatenate(
                [part if k in own and j == 1 else zrow for k in range(4) for j in range(3)], axis=1
            )
            for part in bias_parts
        ]
        return jnp.concatenate(lines + [jnp.zeros((13, 12 * chans), F32)], axis=0).astype(BF16)

    back_weight[...] = jnp.concatenate([upper_rows, lower_rows, bias_rows((1, 2))], axis=0)
    edge_weight[0] = jnp.concatenate([upper_rows, bias_rows((1,))], axis=0)
    edge_weight[1] = jnp.concatenate([lower_rows, bias_rows((2,))], axis=0)

    wide = jnp.concatenate(
        [
            jnp.concatenate([weight_ref[k, j] for j in range(3)] + [zeros], axis=1)
            for k in range(3)
        ]
        + [jnp.zeros((chans, 4 * chans), F32)],
        axis=0,
    )
    fore = wide.T[: 3 * chans]
    fore = jnp.concatenate([fore, pltpu.roll(fore, chans, 1)], axis=0)
    for ref, value in ((box_weight, fore), (rad_weight, jnp.abs(fore))):
        high, low = split2(value)
        ref[...] = jnp.concatenate([high, low, high], axis=1)

    for d in range(2):
        @pl.when(sends[d])
        def _():
            for s in range(first):
                row_copy(d, s).start()

    eye = lax.broadcasted_iota(jnp.int32, (chans, chans), 0) == lax.broadcasted_iota(
        jnp.int32, (chans, chans), 1
    )
    bias_col[...] = jnp.broadcast_to(
        jnp.sum(jnp.where(eye, jnp.broadcast_to(bias_row, (chans, chans)), 0.0), axis=1, keepdims=True),
        (chans, 128),
    )

    where_in_table = (
        lax.broadcasted_iota(jnp.int32, table_ref.shape, 0) * 128
        + lax.broadcasted_iota(jnp.int32, table_ref.shape, 1)
    )
    for s in range(specs):
        table_vec[pl.ds(s, 1), :] = jnp.sum(
            jnp.where(where_in_table == ids_ref[s], table_ref[...], 0.0), axis=0, keepdims=True
        )

    def field(four_rows, weight):
        high, low = split2(four_rows)
        return jnp.dot(
            weight, jnp.concatenate([high, high, low], axis=0), preferred_element_type=F32
        )

    def relax(h, c_res, r_res):
        blocks = [slice(j * chans, (j + 1) * chans) for j in range(3)]
        center_out = combine(*(c_res[b] for b in blocks)) + bias_col[:, :1]
        radius_out = combine(*(r_res[b] for b in blocks))
        upper = center_out + radius_out
        lower = center_out - radius_out
        spread = 2.0 * radius_out
        relaxed = jnp.minimum(jnp.maximum(upper, 0.0), spread) / spread
        state = status[h]
        slope = jnp.where(state == 2, relaxed, jnp.where(state == 1, 1.0, 0.0))
        slopes[h] = slope.astype(BF16)
        cut = jnp.where(state == 2, -relaxed * jnp.minimum(lower, 0.0), 0.0)
        icept[h] = cut.astype(BF16).astype(F32)
        low_end[h] = center[h + 1] - radius[h + 1]
        high_end[h] = center[h + 1] + radius[h + 1]

    loads[2].wait()
    pairs = (rows - 2) // 2

    def inner_slopes(p):
        h = 1 + 2 * p
        four = lambda ref: ref[pl.ds(h, 4)].reshape(4 * chans, cols)
        c_res = field(four(center), box_weight[...])
        r_res = field(four(radius), rad_weight[...])
        for r in range(2):
            block = slice(3 * chans * r, 3 * chans * (r + 1))
            relax(h + r, c_res[block], r_res[block])

    inner_slopes(0)
    for d in range(2):
        @pl.when(exists[d])
        def _():
            box_copy(d).wait_recv()
            pass_copy(d).start()
    inner_slopes(1)
    for d in range(2):
        @pl.when(exists[d])
        def _():
            pass_copy(d).wait()

    blank = jnp.zeros((chans, cols), F32)
    for d, ref_row in ((0, 0), (1, rows - 1)):
        def three(a, ref):
            own = [ref[1], ref[2]] if d == 0 else [ref[rows - 1], ref[rows]]
            halo = [halo_box[d, a].astype(F32)]
            return jnp.concatenate((halo + own if d == 0 else own + halo) + [blank], axis=0)

        c_res = field(three(0, center), box_weight[pl.ds(0, 3 * chans)])
        r_res = field(three(1, radius), rad_weight[pl.ds(0, 3 * chans)])
        relax(ref_row, c_res, r_res)

    for d in range(2):
        @pl.when(sends[d])
        def _():
            slope_copy(d).start()
            for s in range(first, specs):
                row_copy(d, s).start()
    for p in range(2, pairs):
        inner_slopes(p)

    def finish(s, h, value):
        out_ref[s, h] = value.astype(BF16)
        return fold(jnp.minimum(value * low_end[h], value * high_end[h]))

    lane = lax.broadcasted_iota(jnp.int32, (chans, 128), 1)

    def shifts(pre):
        none = jnp.zeros((chans, 128), BF16)
        ahead = pltpu.roll(pre, cols - 1, 1)
        ahead = jnp.concatenate(
            [ahead[:, :-128], jnp.where(lane == 127, none, ahead[:, -128:])], axis=1
        )
        behind = pltpu.roll(pre, 1, 1)
        behind = jnp.concatenate(
            [jnp.where(lane == 0, none, behind[:, :128]), behind[:, 128:]], axis=1
        )
        return ahead, pre, behind

    def edge_row(s, d, halo):
        h = 0 if d == 0 else rows - 1
        own = pl.ds(0, 3) if d == 0 else pl.ds(rows - 3, 3)
        near = shifted[s, own].reshape(9 * chans, cols)
        four = jnp.concatenate([*halo, near] if d == 0 else [near, *halo], axis=0)
        result = jnp.dot(edge_weight[d], four, preferred_element_type=F32)
        acc[s] += finish(s, h, result[:chans]) + fold(result[chans:])

    for copy in coeff_loads:
        copy.wait()

    def inner(s, carry):
        total = jnp.zeros((8, cols), F32)
        for h in range(rows):
            block = coeff[s, h]
            for j, moved in enumerate(shifts(block * slopes[h])):
                shifted[s, h, j] = moved
            total += fold(jnp.minimum(block, 0).astype(F32) * icept[h])
        for p in range(pairs):
            h = 1 + 2 * p
            pre = shifted[s, pl.ds(h - 1, 4)].reshape(12 * chans, cols)
            result = jnp.dot(back_weight[...], pre, preferred_element_type=F32)
            for r in range(2):
                total += finish(s, h + r, result[chans * r : chans * (r + 1)])
            total += fold(result[2 * chans :])
        acc[s] = total
        return carry

    lax.fori_loop(0, specs // 2, inner, 0)
    for d in range(2):
        @pl.when(exists[d])
        def _():
            slope_copy(d).wait_recv()
            spass_copy(d).start()
    lax.fori_loop(specs // 2, specs, inner, 0)

    for d in range(2):
        @pl.when(jnp.logical_not(exists[d]))
        def _():
            def at_border(s, carry):
                edge_row(s, d, [jnp.zeros((3 * chans, cols), BF16)])
                return carry

            lax.fori_loop(0, specs, at_border, 0)

    for d in range(2):
        @pl.when(exists[d])
        def _():
            spass_copy(d).wait()

            def at_halo(s, carry):
                row_copy(d, s).wait_recv()
                edge_row(s, d, shifts(halo_coeff[d, s] * edge_slopes[d]))
                return carry

            lax.fori_loop(0, specs, at_halo, 0)

    folded = jnp.sum(acc[...], axis=1)
    share = folded[:, :128]
    for t in range(1, cols // 128):
        share += folded[:, 128 * t : 128 * (t + 1)]
    parts[0] = share

    def part_copy(step):
        return pltpu.make_async_remote_copy(
            src_ref=parts.at[0],
            dst_ref=parts.at[step],
            send_sem=part_send.at[step],
            recv_sem=part_recv.at[step],
            device_id={"rows": lax.rem(me + step, n_rows)},
            device_id_type=MESH,
        )

    for step in range(1, n_rows):
        part_copy(step).start()
    for d in range(2):
        @pl.when(sends[d])
        def _():
            box_copy(d).wait_send()
            slope_copy(d).wait_send()
            for s in range(specs):
                row_copy(d, s).wait_send()
    for step in range(1, n_rows):
        part_copy(step).wait()
    total = parts[0]
    for step in range(1, n_rows):
        total += parts[step]
    bound = jnp.sum(
        total * (1.0 / (rows * n_rows * cols)) + table_vec[...], axis=1, keepdims=True
    )
    shape = (specs, 128)
    diagonal = lax.broadcasted_iota(jnp.int32, shape, 0) == lax.broadcasted_iota(
        jnp.int32, shape, 1
    )
    line = jnp.sum(jnp.where(diagonal, jnp.broadcast_to(bound, shape), 0.0), axis=0, keepdims=True)
    bounds_ref[...] = line[:, :specs]


def store_kernel(out_vmem, bounds_vmem, out_hbm, bounds_hbm, sem):
    specs = out_vmem.shape[0]
    copies = [
        pltpu.make_async_copy(out_vmem.at[s], out_hbm.at[s], sem.at[s]) for s in range(specs)
    ]
    copies.append(pltpu.make_async_copy(bounds_vmem, bounds_hbm, sem.at[specs]))
    for copy in copies:
        copy.start()
    for copy in copies:
        copy.wait()


def per_device(
    center, radius, conv_weight, conv_bias, split_status, out_coeffs, spec_ids, spec_offsets
):
    n_rows = lax.axis_size("rows")
    specs, rows, cols, chans = out_coeffs.shape
    swap3 = lambda x: jnp.transpose(x, (0, 2, 1))
    dma = pltpu.SemaphoreType.DMA
    vmem = pl.BlockSpec(memory_space=pltpu.VMEM)
    out, bounds = pl.pallas_call(
        functools.partial(kernel, n_rows),
        out_shape=(
            pltpu.VMEM((specs, rows, chans, cols), BF16),
            pltpu.VMEM((1, specs), F32),
        ),
        in_specs=[
            pl.BlockSpec(memory_space=pltpu.HBM),
        ] * 8,
        out_specs=(vmem, vmem),
        scratch_shapes=[
            pltpu.VMEM((rows + 2, chans, cols), F32),
            pltpu.VMEM((rows + 2, chans, cols), F32),
            pltpu.VMEM((rows, chans, cols), jnp.int32),
            pltpu.VMEM((specs, rows, chans, cols), BF16),
            pltpu.VMEM(conv_weight.shape, F32),
            pltpu.VMEM((1, chans), F32),
            pltpu.SMEM((specs,), jnp.int32),
            pltpu.VMEM((spec_offsets.shape[0] // 128, 128), F32),
            pltpu.VMEM((rows, chans, cols), F32),
            pltpu.VMEM((rows, chans, cols), F32),
            pltpu.VMEM((rows, chans, cols), BF16),
            pltpu.VMEM((rows, chans, cols), F32),
            pltpu.VMEM((2, chans, cols), BF16),
            pltpu.VMEM((2, 2, chans, cols), BF16),
            pltpu.VMEM((2, 2, chans, cols), BF16),
            pltpu.VMEM((2, specs, chans, cols), BF16),
            pltpu.VMEM((specs, rows, 3, chans, cols), BF16),
            pltpu.VMEM((6 * chans, 12 * chans), BF16),
            pltpu.VMEM((6 * chans, 12 * chans), BF16),
            pltpu.VMEM((2 * chans + 16, 12 * chans), BF16),
            pltpu.VMEM((2, chans + 16, 12 * chans), BF16),
            pltpu.VMEM((chans, 128), F32),
            pltpu.VMEM((specs, 8, cols), F32),
            pltpu.VMEM((n_rows, specs, 128), F32),
            pltpu.VMEM((specs, 128), F32),
            dma((7,)), dma((specs,)),
            dma((2,)), dma((2,)), dma((2,)), dma((2,)),
            dma((2,)), dma((2,)), dma((2,)), dma((2,)),
            dma((2, specs)), dma((2, specs)), dma((n_rows,)), dma((n_rows,)),
        ],
        compiler_params=pltpu.CompilerParams(
            collective_id=0, has_side_effects=True, vmem_limit_bytes=48 * 1024 * 1024
        ),
        name="bound_pass",
    )(
        *(
            pltpu.with_memory_space_constraint(x, pltpu.HBM)
            for x in (
                swap3(center),
                swap3(radius),
                conv_weight,
                conv_bias.reshape(1, chans),
                swap3(split_status),
                jnp.transpose(out_coeffs, (0, 1, 3, 2)),
                spec_ids,
                spec_offsets.reshape(-1, 128),
            )
        )
    )
    hbm = pl.BlockSpec(memory_space=pltpu.HBM)
    out, bounds = pl.pallas_call(
        store_kernel,
        out_shape=(
            jax.ShapeDtypeStruct((specs, rows, chans, cols), BF16),
            jax.ShapeDtypeStruct((1, specs), F32),
        ),
        in_specs=[vmem, vmem],
        out_specs=(hbm, hbm),
        scratch_shapes=[dma((specs + 1,))],
        compiler_params=pltpu.CompilerParams(vmem_limit_bytes=1024 * 1024),
        name="store",
    )(*(pltpu.with_memory_space_constraint(x, pltpu.VMEM) for x in (out, bounds)))
    return jnp.transpose(out, (0, 1, 3, 2)), bounds.reshape(specs)


def solution(mesh):
    in_specs = (
        P("rows", None, None),
        P("rows", None, None),
        P(),
        P(),
        P("rows", None, None),
        P("specs", "rows", None, None),
        P("specs"),
        P(),
    )
    out_specs = (P("specs", "rows", None, None), P("specs"))
    return jax.shard_map(
        per_device, mesh=mesh, in_specs=in_specs, out_specs=out_specs, check_vma=False
    )
```

```python
import functools

import jax
import jax.numpy as jnp
from jax import lax
from jax.experimental import pallas as pl
from jax.experimental.pallas import tpu as pltpu
from jax.sharding import PartitionSpec as P

F32 = jnp.float32
BF16 = jnp.bfloat16
MESH = pl.DeviceIdType.MESH


def split2(value):
    high = value.astype(BF16)
    return high, (value - high.astype(F32)).astype(BF16)


def combine(first, middle, last):
    width = first.shape[1]
    rolled = pltpu.roll(first, 1, 1)
    lane = lax.broadcasted_iota(jnp.int32, (first.shape[0], 128), 1)
    rolled = jnp.concatenate(
        [jnp.where(lane == 0, 0.0, rolled[:, :128]), rolled[:, 128:]], axis=1
    )
    back = pltpu.roll(last, width - 1, 1)
    back = jnp.concatenate(
        [back[:, :-128], jnp.where(lane == 127, 0.0, back[:, -128:])], axis=1
    )
    return rolled + middle + back


def fold(value):
    rows, width = value.shape
    return jnp.sum(value.reshape(rows // 8, 8, width), axis=0)


def kernel(
    n_rows,
    center_hbm, radius_hbm, weight_hbm, bias_hbm, status_hbm, coeff_hbm, ids_hbm, table_hbm,
    out_ref, bounds_ref,
    center, radius, status, coeff, weight_ref, bias_ref, ids_ref, table_ref,
    low_end, high_end, slopes, icept, edge_slopes,
    box_edge, halo_box, halo_coeff, shifted, box_weight, rad_weight, back_weight, edge_weight, bias_col,
    acc, parts, table_vec,
    load_sem, coeff_sem, box_send, box_recv, pass_send, pass_recv,
    slope_send, slope_recv, spass_send, spass_recv, row_send, row_recv, part_send, part_recv,
):
    specs, rows, chans, cols = coeff.shape
    half = chans // 2
    me = lax.axis_index("rows")
    lane_dev = lax.axis_index("specs")
    core = lax.rem(lane_dev, 2)
    partner = lane_dev + 1 - 2 * core
    has_prev = me > 0
    has_next = me < n_rows - 1
    mine = pl.ds(pl.multiple_of(core * half, half), half)
    exists = (has_prev, has_next)
    sends = (has_next, has_prev)
    target = (me + 1, me - 1)
    edge = (rows - 1, 0)

    loads = [
        pltpu.make_async_copy(center_hbm, center.at[pl.ds(1, rows)], load_sem.at[0]),
        pltpu.make_async_copy(radius_hbm, radius.at[pl.ds(1, rows)], load_sem.at[1]),
        pltpu.make_async_copy(status_hbm, status, load_sem.at[2]),
    ]
    small = [
        pltpu.make_async_copy(weight_hbm, weight_ref, load_sem.at[3]),
        pltpu.make_async_copy(bias_hbm, bias_ref, load_sem.at[4]),
        pltpu.make_async_copy(ids_hbm, ids_ref, load_sem.at[5]),
        pltpu.make_async_copy(table_hbm, table_ref, load_sem.at[6]),
    ]
    for copy in loads[:2] + small + loads[2:]:
        copy.start()

    barrier = pltpu.get_barrier_semaphore()
    for step in range(1, n_rows):
        pl.semaphore_signal(
            barrier, inc=1, device_id={"rows": lax.rem(me + step, n_rows)}, device_id_type=MESH
        )
    pl.semaphore_signal(barrier, inc=1, device_id={"specs": partner}, device_id_type=MESH)

    for copy in loads[:2]:
        copy.wait()
    for d in range(2):
        for a, ref in enumerate((center, radius)):
            box_edge[d, a] = ref[1 + edge[d]].astype(BF16)
    pl.semaphore_wait(barrier, n_rows)

    def box_copy(d):
        return pltpu.make_async_remote_copy(
            src_ref=box_edge.at[d, :, mine],
            dst_ref=halo_box.at[d, :, mine],
            send_sem=box_send.at[d],
            recv_sem=box_recv.at[d],
            device_id={"rows": target[d]},
            device_id_type=MESH,
        )

    def pass_copy(d):
        return pltpu.make_async_remote_copy(
            src_ref=halo_box.at[d, :, mine],
            dst_ref=halo_box.at[d, :, mine],
            send_sem=pass_send.at[d],
            recv_sem=pass_recv.at[d],
            device_id={"specs": partner},
            device_id_type=MESH,
        )

    def slope_copy(d):
        return pltpu.make_async_remote_copy(
            src_ref=slopes.at[edge[d], mine],
            dst_ref=edge_slopes.at[d, mine],
            send_sem=slope_send.at[d],
            recv_sem=slope_recv.at[d],
            device_id={"rows": target[d]},
            device_id_type=MESH,
        )

    def spass_copy(d):
        return pltpu.make_async_remote_copy(
            src_ref=edge_slopes.at[d, mine],
            dst_ref=edge_slopes.at[d, mine],
            send_sem=spass_send.at[d],
            recv_sem=spass_recv.at[d],
            device_id={"specs": partner},
            device_id_type=MESH,
        )

    def row_copy(d, s):
        return pltpu.make_async_remote_copy(
            src_ref=coeff_hbm.at[s, edge[d]],
            dst_ref=halo_coeff.at[d, s],
            send_sem=row_send.at[d, s],
            recv_sem=row_recv.at[d, s],
            device_id={"rows": target[d]},
            device_id_type=MESH,
        )

    first = specs // 2
    for d in range(2):
        @pl.when(sends[d])
        def _():
            box_copy(d).start()
            for s in range(first):
                row_copy(d, s).start()

    coeff_loads = [
        pltpu.make_async_copy(coeff_hbm.at[s], coeff.at[s], coeff_sem.at[s]) for s in range(specs)
    ]
    for copy in coeff_loads:
        copy.start()

    for d in range(2):
        @pl.when(jnp.logical_not(exists[d]))
        def _():
            halo_box[d] = jnp.zeros(halo_box.shape[1:], BF16)

    for copy in small:
        copy.wait()

    zeros = jnp.zeros((chans, chans), F32)
    back = jnp.concatenate([weight_ref[2 - k, j] for k in range(3) for j in range(3)], axis=1)
    blank3 = jnp.zeros((chans, 3 * chans), F32)
    upper_rows = jnp.concatenate([back, blank3], axis=1).astype(BF16)
    lower_rows = jnp.concatenate([blank3, back], axis=1).astype(BF16)
    bias_row = bias_ref[...]
    bias_high = bias_row.astype(BF16).astype(F32)
    bias_mid = (bias_row - bias_high).astype(BF16).astype(F32)
    bias_low = bias_row - bias_high - bias_mid
    zrow = jnp.zeros((1, chans), F32)
    bias_parts = (bias_high, bias_mid, bias_low)

    def bias_rows(own):
        lines = [
            jnp.concatenate(
                [part if k in own and j == 1 else zrow for k in range(4) for j in range(3)], axis=1
            )
            for part in bias_parts
        ]
        return jnp.concatenate(lines + [jnp.zeros((13, 12 * chans), F32)], axis=0).astype(BF16)

    back_weight[...] = jnp.concatenate([upper_rows, lower_rows, bias_rows((1, 2))], axis=0)
    edge_weight[0] = jnp.concatenate([upper_rows, bias_rows((1,))], axis=0)
    edge_weight[1] = jnp.concatenate([lower_rows, bias_rows((2,))], axis=0)

    wide = jnp.concatenate(
        [
            jnp.concatenate([weight_ref[k, j] for j in range(3)] + [zeros], axis=1)
            for k in range(3)
        ]
        + [jnp.zeros((chans, 4 * chans), F32)],
        axis=0,
    )
    fore = wide.T[: 3 * chans]
    fore = jnp.concatenate([fore, pltpu.roll(fore, chans, 1)], axis=0)
    high, low = split2(fore)
    box_weight[...] = jnp.concatenate([high, low, high], axis=1)
    rad_weight[...] = jnp.abs(fore).astype(BF16)

    eye = lax.broadcasted_iota(jnp.int32, (chans, chans), 0) == lax.broadcasted_iota(
        jnp.int32, (chans, chans), 1
    )
    bias_col[...] = jnp.broadcast_to(
        jnp.sum(jnp.where(eye, jnp.broadcast_to(bias_row, (chans, chans)), 0.0), axis=1, keepdims=True),
        (chans, 128),
    )

    where_in_table = (
        lax.broadcasted_iota(jnp.int32, table_ref.shape, 0) * 128
        + lax.broadcasted_iota(jnp.int32, table_ref.shape, 1)
    )
    for s in range(specs):
        table_vec[pl.ds(s, 1), :] = jnp.sum(
            jnp.where(where_in_table == ids_ref[s], table_ref[...], 0.0), axis=0, keepdims=True
        )

    def field(four_rows, weight):
        high, low = split2(four_rows)
        return jnp.dot(
            weight, jnp.concatenate([high, high, low], axis=0), preferred_element_type=F32
        )

    def plain(four_rows, weight):
        return jnp.dot(weight, four_rows.astype(BF16), preferred_element_type=F32)

    def relax(h, c_res, r_res):
        blocks = [slice(j * chans, (j + 1) * chans) for j in range(3)]
        center_out = combine(*(c_res[b] for b in blocks)) + bias_col[:, :1]
        radius_out = combine(*(r_res[b] for b in blocks))
        upper = center_out + radius_out
        lower = center_out - radius_out
        spread = 2.0 * radius_out
        relaxed = jnp.minimum(jnp.maximum(upper, 0.0), spread) / spread
        state = status[h]
        slope = jnp.where(state == 2, relaxed, jnp.where(state == 1, 1.0, 0.0))
        slopes[h] = slope.astype(BF16)
        cut = jnp.where(state == 2, -relaxed * jnp.minimum(lower, 0.0), 0.0)
        icept[h] = cut.astype(BF16).astype(F32)
        low_end[h] = center[h + 1] - radius[h + 1]
        high_end[h] = center[h + 1] + radius[h + 1]

    loads[2].wait()
    pairs = (rows - 2) // 2

    def inner_slopes(p):
        h = 1 + 2 * p
        four = lambda ref: ref[pl.ds(h, 4)].reshape(4 * chans, cols)
        c_res = field(four(center), box_weight[...])
        r_res = plain(four(radius), rad_weight[...])
        for r in range(2):
            block = slice(3 * chans * r, 3 * chans * (r + 1))
            relax(h + r, c_res[block], r_res[block])

    inner_slopes(0)
    for d in range(2):
        @pl.when(exists[d])
        def _():
            box_copy(d).wait_recv()
            pass_copy(d).start()
    inner_slopes(1)
    for d in range(2):
        @pl.when(exists[d])
        def _():
            pass_copy(d).wait()

    blank = jnp.zeros((chans, cols), F32)
    for d, ref_row in ((0, 0), (1, rows - 1)):
        def three(a, ref):
            own = [ref[1], ref[2]] if d == 0 else [ref[rows - 1], ref[rows]]
            halo = [halo_box[d, a].astype(F32)]
            return jnp.concatenate((halo + own if d == 0 else own + halo) + [blank], axis=0)

        c_res = field(three(0, center), box_weight[pl.ds(0, 3 * chans)])
        r_res = plain(three(1, radius), rad_weight[pl.ds(0, 3 * chans)])
        relax(ref_row, c_res, r_res)

    for d in range(2):
        @pl.when(sends[d])
        def _():
            slope_copy(d).start()
            for s in range(first, specs):
                row_copy(d, s).start()
    for p in range(2, pairs):
        inner_slopes(p)

    def finish(s, h, value):
        out_ref[s, h] = value.astype(BF16)
        return fold(jnp.minimum(value * low_end[h], value * high_end[h]))

    lane = lax.broadcasted_iota(jnp.int32, (chans, 128), 1)

    def shifts(pre):
        none = jnp.zeros((chans, 128), BF16)
        ahead = pltpu.roll(pre, cols - 1, 1)
        ahead = jnp.concatenate(
            [ahead[:, :-128], jnp.where(lane == 127, none, ahead[:, -128:])], axis=1
        )
        behind = pltpu.roll(pre, 1, 1)
        behind = jnp.concatenate(
            [jnp.where(lane == 0, none, behind[:, :128]), behind[:, 128:]], axis=1
        )
        return ahead, pre, behind

    def edge_row(s, d, halo):
        h = 0 if d == 0 else rows - 1
        own = pl.ds(0, 3) if d == 0 else pl.ds(rows - 3, 3)
        near = shifted[s, own].reshape(9 * chans, cols)
        four = jnp.concatenate([*halo, near] if d == 0 else [near, *halo], axis=0)
        result = jnp.dot(edge_weight[d], four, preferred_element_type=F32)
        acc[s] += finish(s, h, result[:chans]) + fold(result[chans:])

    for copy in coeff_loads:
        copy.wait()

    def inner(s, carry):
        total = jnp.zeros((8, cols), F32)
        for h in range(rows):
            block = coeff[s, h]
            for j, moved in enumerate(shifts(block * slopes[h])):
                shifted[s, h, j] = moved
            total += fold(jnp.minimum(block, 0).astype(F32) * icept[h])
        for p in range(pairs):
            h = 1 + 2 * p
            pre = shifted[s, pl.ds(h - 1, 4)].reshape(12 * chans, cols)
            result = jnp.dot(back_weight[...], pre, preferred_element_type=F32)
            for r in range(2):
                total += finish(s, h + r, result[chans * r : chans * (r + 1)])
            total += fold(result[2 * chans :])
        acc[s] = total
        return carry

    lax.fori_loop(0, specs // 2, inner, 0)
    for d in range(2):
        @pl.when(exists[d])
        def _():
            slope_copy(d).wait_recv()
            spass_copy(d).start()
    lax.fori_loop(specs // 2, specs, inner, 0)

    for d in range(2):
        @pl.when(jnp.logical_not(exists[d]))
        def _():
            def at_border(s, carry):
                edge_row(s, d, [jnp.zeros((3 * chans, cols), BF16)])
                return carry

            lax.fori_loop(0, specs, at_border, 0)

    for d in range(2):
        @pl.when(exists[d])
        def _():
            spass_copy(d).wait()

            def at_halo(s, carry):
                row_copy(d, s).wait_recv()
                edge_row(s, d, shifts(halo_coeff[d, s] * edge_slopes[d]))
                return carry

            lax.fori_loop(0, specs, at_halo, 0)

    folded = jnp.sum(acc[...], axis=1)
    share = folded[:, :128]
    for t in range(1, cols // 128):
        share += folded[:, 128 * t : 128 * (t + 1)]
    parts[0] = share

    def part_copy(step):
        return pltpu.make_async_remote_copy(
            src_ref=parts.at[0],
            dst_ref=parts.at[step],
            send_sem=part_send.at[step],
            recv_sem=part_recv.at[step],
            device_id={"rows": lax.rem(me + step, n_rows)},
            device_id_type=MESH,
        )

    for step in range(1, n_rows):
        part_copy(step).start()
    for d in range(2):
        @pl.when(sends[d])
        def _():
            box_copy(d).wait_send()
            slope_copy(d).wait_send()
            for s in range(specs):
                row_copy(d, s).wait_send()
    for step in range(1, n_rows):
        part_copy(step).wait()
    total = parts[0]
    for step in range(1, n_rows):
        total += parts[step]
    bound = jnp.sum(
        total * (1.0 / (rows * n_rows * cols)) + table_vec[...], axis=1, keepdims=True
    )
    shape = (specs, 128)
    diagonal = lax.broadcasted_iota(jnp.int32, shape, 0) == lax.broadcasted_iota(
        jnp.int32, shape, 1
    )
    line = jnp.sum(jnp.where(diagonal, jnp.broadcast_to(bound, shape), 0.0), axis=0, keepdims=True)
    bounds_ref[...] = line[:, :specs]


def store_kernel(out_vmem, bounds_vmem, out_hbm, bounds_hbm, sem):
    specs = out_vmem.shape[0]
    copies = [
        pltpu.make_async_copy(out_vmem.at[s], out_hbm.at[s], sem.at[s]) for s in range(specs)
    ]
    copies.append(pltpu.make_async_copy(bounds_vmem, bounds_hbm, sem.at[specs]))
    for copy in copies:
        copy.start()
    for copy in copies:
        copy.wait()


def per_device(
    center, radius, conv_weight, conv_bias, split_status, out_coeffs, spec_ids, spec_offsets
):
    n_rows = lax.axis_size("rows")
    specs, rows, cols, chans = out_coeffs.shape
    swap3 = lambda x: jnp.transpose(x, (0, 2, 1))
    dma = pltpu.SemaphoreType.DMA
    vmem = pl.BlockSpec(memory_space=pltpu.VMEM)
    out, bounds = pl.pallas_call(
        functools.partial(kernel, n_rows),
        out_shape=(
            pltpu.VMEM((specs, rows, chans, cols), BF16),
            pltpu.VMEM((1, specs), F32),
        ),
        in_specs=[
            pl.BlockSpec(memory_space=pltpu.HBM),
        ] * 8,
        out_specs=(vmem, vmem),
        scratch_shapes=[
            pltpu.VMEM((rows + 2, chans, cols), F32),
            pltpu.VMEM((rows + 2, chans, cols), F32),
            pltpu.VMEM((rows, chans, cols), jnp.int32),
            pltpu.VMEM((specs, rows, chans, cols), BF16),
            pltpu.VMEM(conv_weight.shape, F32),
            pltpu.VMEM((1, chans), F32),
            pltpu.SMEM((specs,), jnp.int32),
            pltpu.VMEM((spec_offsets.shape[0] // 128, 128), F32),
            pltpu.VMEM((rows, chans, cols), F32),
            pltpu.VMEM((rows, chans, cols), F32),
            pltpu.VMEM((rows, chans, cols), BF16),
            pltpu.VMEM((rows, chans, cols), F32),
            pltpu.VMEM((2, chans, cols), BF16),
            pltpu.VMEM((2, 2, chans, cols), BF16),
            pltpu.VMEM((2, 2, chans, cols), BF16),
            pltpu.VMEM((2, specs, chans, cols), BF16),
            pltpu.VMEM((specs, rows, 3, chans, cols), BF16),
            pltpu.VMEM((6 * chans, 12 * chans), BF16),
            pltpu.VMEM((6 * chans, 4 * chans), BF16),
            pltpu.VMEM((2 * chans + 16, 12 * chans), BF16),
            pltpu.VMEM((2, chans + 16, 12 * chans), BF16),
            pltpu.VMEM((chans, 128), F32),
            pltpu.VMEM((specs, 8, cols), F32),
            pltpu.VMEM((n_rows, specs, 128), F32),
            pltpu.VMEM((specs, 128), F32),
            dma((7,)), dma((specs,)),
            dma((2,)), dma((2,)), dma((2,)), dma((2,)),
            dma((2,)), dma((2,)), dma((2,)), dma((2,)),
            dma((2, specs)), dma((2, specs)), dma((n_rows,)), dma((n_rows,)),
        ],
        compiler_params=pltpu.CompilerParams(
            collective_id=0, has_side_effects=True, vmem_limit_bytes=48 * 1024 * 1024
        ),
        name="bound_pass",
    )(
        *(
            pltpu.with_memory_space_constraint(x, pltpu.HBM)
            for x in (
                swap3(center),
                swap3(radius),
                conv_weight,
                conv_bias.reshape(1, chans),
                swap3(split_status),
                jnp.transpose(out_coeffs, (0, 1, 3, 2)),
                spec_ids,
                spec_offsets.reshape(-1, 128),
            )
        )
    )
    hbm = pl.BlockSpec(memory_space=pltpu.HBM)
    out, bounds = pl.pallas_call(
        store_kernel,
        out_shape=(
            jax.ShapeDtypeStruct((specs, rows, chans, cols), BF16),
            jax.ShapeDtypeStruct((1, specs), F32),
        ),
        in_specs=[vmem, vmem],
        out_specs=(hbm, hbm),
        scratch_shapes=[dma((specs + 1,))],
        compiler_params=pltpu.CompilerParams(vmem_limit_bytes=1024 * 1024),
        name="store",
    )(*(pltpu.with_memory_space_constraint(x, pltpu.VMEM) for x in (out, bounds)))
    return jnp.transpose(out, (0, 1, 3, 2)), bounds.reshape(specs)


def solution(mesh):
    in_specs = (
        P("rows", None, None),
        P("rows", None, None),
        P(),
        P(),
        P("rows", None, None),
        P("specs", "rows", None, None),
        P("specs"),
        P(),
    )
    out_specs = (P("specs", "rows", None, None), P("specs"))
    return jax.shard_map(
        per_device, mesh=mesh, in_specs=in_specs, out_specs=out_specs, check_vma=False
    )
```

```python
import functools

import jax
import jax.numpy as jnp
from jax import lax
from jax.experimental import pallas as pl
from jax.experimental.pallas import tpu as pltpu
from jax.sharding import PartitionSpec as P

F32 = jnp.float32
BF16 = jnp.bfloat16
MESH = pl.DeviceIdType.MESH


def split2(value):
    high = value.astype(BF16)
    return high, (value - high.astype(F32)).astype(BF16)


def combine(first, middle, last):
    width = first.shape[1]
    rolled = pltpu.roll(first, 1, 1)
    lane = lax.broadcasted_iota(jnp.int32, (first.shape[0], 128), 1)
    rolled = jnp.concatenate(
        [jnp.where(lane == 0, 0.0, rolled[:, :128]), rolled[:, 128:]], axis=1
    )
    back = pltpu.roll(last, width - 1, 1)
    back = jnp.concatenate(
        [back[:, :-128], jnp.where(lane == 127, 0.0, back[:, -128:])], axis=1
    )
    return rolled + middle + back


def fold(value):
    rows, width = value.shape
    return jnp.sum(value.reshape(rows // 8, 8, width), axis=0)


def kernel(
    n_rows,
    center_hbm, radius_hbm, weight_hbm, bias_hbm, status_hbm, coeff_hbm, ids_hbm, table_hbm,
    out_ref, bounds_ref,
    center, radius, status, coeff, weight_ref, bias_ref, ids_ref, table_ref,
    low_end, high_end, slopes, icept, edge_slopes,
    box_edge, halo_box, halo_coeff, shifted, box_weight, rad_weight, back_weight, edge_weight, bias_col,
    acc, parts, table_vec,
    load_sem, coeff_sem, box_send, box_recv, pass_send, pass_recv,
    slope_send, slope_recv, spass_send, spass_recv, row_send, row_recv, part_send, part_recv,
):
    specs, rows, chans, cols = coeff.shape
    half = chans // 2
    me = lax.axis_index("rows")
    lane_dev = lax.axis_index("specs")
    core = lax.rem(lane_dev, 2)
    partner = lane_dev + 1 - 2 * core
    has_prev = me > 0
    has_next = me < n_rows - 1
    mine = pl.ds(pl.multiple_of(core * half, half), half)
    exists = (has_prev, has_next)
    sends = (has_next, has_prev)
    target = (me + 1, me - 1)
    edge = (rows - 1, 0)

    loads = [
        pltpu.make_async_copy(center_hbm, center.at[pl.ds(1, rows)], load_sem.at[0]),
        pltpu.make_async_copy(radius_hbm, radius.at[pl.ds(1, rows)], load_sem.at[1]),
        pltpu.make_async_copy(status_hbm, status, load_sem.at[2]),
    ]
    small = [
        pltpu.make_async_copy(weight_hbm, weight_ref, load_sem.at[3]),
        pltpu.make_async_copy(bias_hbm, bias_ref, load_sem.at[4]),
        pltpu.make_async_copy(ids_hbm, ids_ref, load_sem.at[5]),
        pltpu.make_async_copy(table_hbm, table_ref, load_sem.at[6]),
    ]
    for copy in loads[:2] + small + loads[2:]:
        copy.start()

    barrier = pltpu.get_barrier_semaphore()
    for step in range(1, n_rows):
        pl.semaphore_signal(
            barrier, inc=1, device_id={"rows": lax.rem(me + step, n_rows)}, device_id_type=MESH
        )
    pl.semaphore_signal(barrier, inc=1, device_id={"specs": partner}, device_id_type=MESH)

    for copy in loads[:2]:
        copy.wait()
    for d in range(2):
        for a, ref in enumerate((center, radius)):
            box_edge[d, a] = ref[1 + edge[d]].astype(BF16)
    pl.semaphore_wait(barrier, n_rows)

    def box_copy(d):
        return pltpu.make_async_remote_copy(
            src_ref=box_edge.at[d, :, mine],
            dst_ref=halo_box.at[d, :, mine],
            send_sem=box_send.at[d],
            recv_sem=box_recv.at[d],
            device_id={"rows": target[d]},
            device_id_type=MESH,
        )

    def pass_copy(d):
        return pltpu.make_async_remote_copy(
            src_ref=halo_box.at[d, :, mine],
            dst_ref=halo_box.at[d, :, mine],
            send_sem=pass_send.at[d],
            recv_sem=pass_recv.at[d],
            device_id={"specs": partner},
            device_id_type=MESH,
        )

    def slope_copy(d):
        return pltpu.make_async_remote_copy(
            src_ref=slopes.at[edge[d], mine],
            dst_ref=edge_slopes.at[d, mine],
            send_sem=slope_send.at[d],
            recv_sem=slope_recv.at[d],
            device_id={"rows": target[d]},
            device_id_type=MESH,
        )

    def spass_copy(d):
        return pltpu.make_async_remote_copy(
            src_ref=edge_slopes.at[d, mine],
            dst_ref=edge_slopes.at[d, mine],
            send_sem=spass_send.at[d],
            recv_sem=spass_recv.at[d],
            device_id={"specs": partner},
            device_id_type=MESH,
        )

    def row_copy(d, s):
        return pltpu.make_async_remote_copy(
            src_ref=coeff_hbm.at[s, edge[d]],
            dst_ref=halo_coeff.at[d, s],
            send_sem=row_send.at[d, s],
            recv_sem=row_recv.at[d, s],
            device_id={"rows": target[d]},
            device_id_type=MESH,
        )

    first = specs * 5 // 8
    for d in range(2):
        @pl.when(sends[d])
        def _():
            box_copy(d).start()
            for s in range(first):
                row_copy(d, s).start()

    coeff_loads = [
        pltpu.make_async_copy(coeff_hbm.at[s], coeff.at[s], coeff_sem.at[s]) for s in range(specs)
    ]
    for copy in coeff_loads:
        copy.start()

    for d in range(2):
        @pl.when(jnp.logical_not(exists[d]))
        def _():
            halo_box[d] = jnp.zeros(halo_box.shape[1:], BF16)

    for copy in small:
        copy.wait()

    zeros = jnp.zeros((chans, chans), F32)
    back = jnp.concatenate([weight_ref[2 - k, j] for k in range(3) for j in range(3)], axis=1)
    blank3 = jnp.zeros((chans, 3 * chans), F32)
    upper_rows = jnp.concatenate([back, blank3], axis=1).astype(BF16)
    lower_rows = jnp.concatenate([blank3, back], axis=1).astype(BF16)
    bias_row = bias_ref[...]
    bias_high = bias_row.astype(BF16).astype(F32)
    bias_mid = (bias_row - bias_high).astype(BF16).astype(F32)
    bias_low = bias_row - bias_high - bias_mid
    zrow = jnp.zeros((1, chans), F32)
    bias_parts = (bias_high, bias_mid, bias_low)

    def bias_rows(own):
        lines = [
            jnp.concatenate(
                [part if k in own and j == 1 else zrow for k in range(4) for j in range(3)], axis=1
            )
            for part in bias_parts
        ]
        return jnp.concatenate(lines + [jnp.zeros((13, 12 * chans), F32)], axis=0).astype(BF16)

    back_weight[...] = jnp.concatenate([upper_rows, lower_rows, bias_rows((1, 2))], axis=0)
    edge_weight[0] = jnp.concatenate([upper_rows, bias_rows((1,))], axis=0)
    edge_weight[1] = jnp.concatenate([lower_rows, bias_rows((2,))], axis=0)

    wide = jnp.concatenate(
        [
            jnp.concatenate([weight_ref[k, j] for j in range(3)] + [zeros], axis=1)
            for k in range(3)
        ]
        + [jnp.zeros((chans, 4 * chans), F32)],
        axis=0,
    )
    fore = wide.T[: 3 * chans]
    fore = jnp.concatenate([fore, pltpu.roll(fore, chans, 1)], axis=0)
    high, low = split2(fore)
    box_weight[...] = jnp.concatenate([high, low, high], axis=1)
    rad_weight[...] = jnp.abs(fore).astype(BF16)

    eye = lax.broadcasted_iota(jnp.int32, (chans, chans), 0) == lax.broadcasted_iota(
        jnp.int32, (chans, chans), 1
    )
    bias_col[...] = jnp.broadcast_to(
        jnp.sum(jnp.where(eye, jnp.broadcast_to(bias_row, (chans, chans)), 0.0), axis=1, keepdims=True),
        (chans, 128),
    )

    where_in_table = (
        lax.broadcasted_iota(jnp.int32, table_ref.shape, 0) * 128
        + lax.broadcasted_iota(jnp.int32, table_ref.shape, 1)
    )
    for s in range(specs):
        table_vec[pl.ds(s, 1), :] = jnp.sum(
            jnp.where(where_in_table == ids_ref[s], table_ref[...], 0.0), axis=0, keepdims=True
        )

    def field(four_rows, weight):
        high, low = split2(four_rows)
        return jnp.dot(
            weight, jnp.concatenate([high, high, low], axis=0), preferred_element_type=F32
        )

    def plain(four_rows, weight):
        return jnp.dot(weight, four_rows.astype(BF16), preferred_element_type=F32)

    def relax(h, c_res, r_res):
        blocks = [slice(j * chans, (j + 1) * chans) for j in range(3)]
        center_out = combine(*(c_res[b] for b in blocks)) + bias_col[:, :1]
        radius_out = combine(*(r_res[b] for b in blocks))
        upper = center_out + radius_out
        lower = center_out - radius_out
        spread = 2.0 * radius_out
        relaxed = jnp.minimum(jnp.maximum(upper, 0.0), spread) / spread
        state = status[h]
        slope = jnp.where(state == 2, relaxed, jnp.where(state == 1, 1.0, 0.0))
        slopes[h] = slope.astype(BF16)
        cut = jnp.where(state == 2, -relaxed * jnp.minimum(lower, 0.0), 0.0)
        icept[h] = cut.astype(BF16).astype(F32)
        low_end[h] = center[h + 1] - radius[h + 1]
        high_end[h] = center[h + 1] + radius[h + 1]

    loads[2].wait()
    pairs = (rows - 2) // 2

    def inner_slopes(p):
        h = 1 + 2 * p
        four = lambda ref: ref[pl.ds(h, 4)].reshape(4 * chans, cols)
        c_res = field(four(center), box_weight[...])
        r_res = plain(four(radius), rad_weight[...])
        for r in range(2):
            block = slice(3 * chans * r, 3 * chans * (r + 1))
            relax(h + r, c_res[block], r_res[block])

    for p in range(pairs):
        inner_slopes(p)

    def finish(s, h, value):
        out_ref[s, h] = value.astype(BF16)
        return fold(jnp.minimum(value * low_end[h], value * high_end[h]))

    lane = lax.broadcasted_iota(jnp.int32, (chans, 128), 1)

    def shifts(pre):
        none = jnp.zeros((chans, 128), BF16)
        ahead = pltpu.roll(pre, cols - 1, 1)
        ahead = jnp.concatenate(
            [ahead[:, :-128], jnp.where(lane == 127, none, ahead[:, -128:])], axis=1
        )
        behind = pltpu.roll(pre, 1, 1)
        behind = jnp.concatenate(
            [jnp.where(lane == 0, none, behind[:, :128]), behind[:, 128:]], axis=1
        )
        return ahead, pre, behind

    def edge_row(s, d, halo):
        h = 0 if d == 0 else rows - 1
        own = pl.ds(0, 3) if d == 0 else pl.ds(rows - 3, 3)
        near = shifted[s, own].reshape(9 * chans, cols)
        four = jnp.concatenate([*halo, near] if d == 0 else [near, *halo], axis=0)
        result = jnp.dot(edge_weight[d], four, preferred_element_type=F32)
        acc[s] += finish(s, h, result[:chans]) + fold(result[chans:])

    for copy in coeff_loads:
        copy.wait()

    def rows_and_pairs(s, total, own_rows, own_pairs):
        for h in own_rows:
            block = coeff[s, h]
            for j, moved in enumerate(shifts(block * slopes[h])):
                shifted[s, h, j] = moved
            total += fold(jnp.minimum(block, 0).astype(F32) * icept[h])
        for p in own_pairs:
            h = 1 + 2 * p
            pre = shifted[s, pl.ds(h - 1, 4)].reshape(12 * chans, cols)
            result = jnp.dot(back_weight[...], pre, preferred_element_type=F32)
            for r in range(2):
                total += finish(s, h + r, result[chans * r : chans * (r + 1)])
            total += fold(result[2 * chans :])
        acc[s] = total

    def inside(s, carry):
        blank_total = jnp.zeros((8, cols), F32)
        rows_and_pairs(s, blank_total, range(1, rows - 1), range(1, pairs - 1))
        return carry

    def outside(s, carry):
        rows_and_pairs(s, acc[s], (0, rows - 1), sorted({0, pairs - 1}))
        return carry

    for d in range(2):
        @pl.when(exists[d])
        def _():
            box_copy(d).wait_recv()
            pass_copy(d).start()
    lax.fori_loop(0, specs // 2, inside, 0)
    for d in range(2):
        @pl.when(exists[d])
        def _():
            pass_copy(d).wait()

    blank = jnp.zeros((chans, cols), F32)
    for d, ref_row in ((0, 0), (1, rows - 1)):
        def three(a, ref):
            own = [ref[1], ref[2]] if d == 0 else [ref[rows - 1], ref[rows]]
            halo = [halo_box[d, a].astype(F32)]
            return jnp.concatenate((halo + own if d == 0 else own + halo) + [blank], axis=0)

        c_res = field(three(0, center), box_weight[pl.ds(0, 3 * chans)])
        r_res = plain(three(1, radius), rad_weight[pl.ds(0, 3 * chans)])
        relax(ref_row, c_res, r_res)

    for d in range(2):
        @pl.when(sends[d])
        def _():
            slope_copy(d).start()
            for s in range(first, specs):
                row_copy(d, s).start()
    lax.fori_loop(specs // 2, specs, inside, 0)
    lax.fori_loop(0, specs // 2, outside, 0)
    for d in range(2):
        @pl.when(exists[d])
        def _():
            slope_copy(d).wait_recv()
            spass_copy(d).start()
    lax.fori_loop(specs // 2, specs, outside, 0)
    for d in range(2):
        @pl.when(jnp.logical_not(exists[d]))
        def _():
            def at_border(s, carry):
                edge_row(s, d, [jnp.zeros((3 * chans, cols), BF16)])
                return carry

            lax.fori_loop(0, specs, at_border, 0)

    for d in range(2):
        @pl.when(exists[d])
        def _():
            spass_copy(d).wait()

            def at_halo(s, carry):
                row_copy(d, s).wait_recv()
                edge_row(s, d, shifts(halo_coeff[d, s] * edge_slopes[d]))
                return carry

            lax.fori_loop(0, specs, at_halo, 0)

    folded = jnp.sum(acc[...], axis=1)
    share = folded[:, :128]
    for t in range(1, cols // 128):
        share += folded[:, 128 * t : 128 * (t + 1)]
    parts[0] = share

    def part_copy(step):
        return pltpu.make_async_remote_copy(
            src_ref=parts.at[0],
            dst_ref=parts.at[step],
            send_sem=part_send.at[step],
            recv_sem=part_recv.at[step],
            device_id={"rows": lax.rem(me + step, n_rows)},
            device_id_type=MESH,
        )

    for step in range(1, n_rows):
        part_copy(step).start()
    for d in range(2):
        @pl.when(sends[d])
        def _():
            box_copy(d).wait_send()
            slope_copy(d).wait_send()
            for s in range(specs):
                row_copy(d, s).wait_send()
    for step in range(1, n_rows):
        part_copy(step).wait()
    total = parts[0]
    for step in range(1, n_rows):
        total += parts[step]
    bound = jnp.sum(
        total * (1.0 / (rows * n_rows * cols)) + table_vec[...], axis=1, keepdims=True
    )
    shape = (specs, 128)
    diagonal = lax.broadcasted_iota(jnp.int32, shape, 0) == lax.broadcasted_iota(
        jnp.int32, shape, 1
    )
    line = jnp.sum(jnp.where(diagonal, jnp.broadcast_to(bound, shape), 0.0), axis=0, keepdims=True)
    bounds_ref[...] = line[:, :specs]


def store_kernel(out_vmem, bounds_vmem, out_hbm, bounds_hbm, sem):
    specs = out_vmem.shape[0]
    copies = [
        pltpu.make_async_copy(out_vmem.at[s], out_hbm.at[s], sem.at[s]) for s in range(specs)
    ]
    copies.append(pltpu.make_async_copy(bounds_vmem, bounds_hbm, sem.at[specs]))
    for copy in copies:
        copy.start()
    for copy in copies:
        copy.wait()


def per_device(
    center, radius, conv_weight, conv_bias, split_status, out_coeffs, spec_ids, spec_offsets
):
    n_rows = lax.axis_size("rows")
    specs, rows, cols, chans = out_coeffs.shape
    swap3 = lambda x: jnp.transpose(x, (0, 2, 1))
    dma = pltpu.SemaphoreType.DMA
    vmem = pl.BlockSpec(memory_space=pltpu.VMEM)
    out, bounds = pl.pallas_call(
        functools.partial(kernel, n_rows),
        out_shape=(
            pltpu.VMEM((specs, rows, chans, cols), BF16),
            pltpu.VMEM((1, specs), F32),
        ),
        in_specs=[
            pl.BlockSpec(memory_space=pltpu.HBM),
        ] * 8,
        out_specs=(vmem, vmem),
        scratch_shapes=[
            pltpu.VMEM((rows + 2, chans, cols), F32),
            pltpu.VMEM((rows + 2, chans, cols), F32),
            pltpu.VMEM((rows, chans, cols), jnp.int32),
            pltpu.VMEM((specs, rows, chans, cols), BF16),
            pltpu.VMEM(conv_weight.shape, F32),
            pltpu.VMEM((1, chans), F32),
            pltpu.SMEM((specs,), jnp.int32),
            pltpu.VMEM((spec_offsets.shape[0] // 128, 128), F32),
            pltpu.VMEM((rows, chans, cols), F32),
            pltpu.VMEM((rows, chans, cols), F32),
            pltpu.VMEM((rows, chans, cols), BF16),
            pltpu.VMEM((rows, chans, cols), F32),
            pltpu.VMEM((2, chans, cols), BF16),
            pltpu.VMEM((2, 2, chans, cols), BF16),
            pltpu.VMEM((2, 2, chans, cols), BF16),
            pltpu.VMEM((2, specs, chans, cols), BF16),
            pltpu.VMEM((specs, rows, 3, chans, cols), BF16),
            pltpu.VMEM((6 * chans, 12 * chans), BF16),
            pltpu.VMEM((6 * chans, 4 * chans), BF16),
            pltpu.VMEM((2 * chans + 16, 12 * chans), BF16),
            pltpu.VMEM((2, chans + 16, 12 * chans), BF16),
            pltpu.VMEM((chans, 128), F32),
            pltpu.VMEM((specs, 8, cols), F32),
            pltpu.VMEM((n_rows, specs, 128), F32),
            pltpu.VMEM((specs, 128), F32),
            dma((7,)), dma((specs,)),
            dma((2,)), dma((2,)), dma((2,)), dma((2,)),
            dma((2,)), dma((2,)), dma((2,)), dma((2,)),
            dma((2, specs)), dma((2, specs)), dma((n_rows,)), dma((n_rows,)),
        ],
        compiler_params=pltpu.CompilerParams(
            collective_id=0, has_side_effects=True, vmem_limit_bytes=48 * 1024 * 1024
        ),
        name="bound_pass",
    )(
        *(
            pltpu.with_memory_space_constraint(x, pltpu.HBM)
            for x in (
                swap3(center),
                swap3(radius),
                conv_weight,
                conv_bias.reshape(1, chans),
                swap3(split_status),
                jnp.transpose(out_coeffs, (0, 1, 3, 2)),
                spec_ids,
                spec_offsets.reshape(-1, 128),
            )
        )
    )
    hbm = pl.BlockSpec(memory_space=pltpu.HBM)
    out, bounds = pl.pallas_call(
        store_kernel,
        out_shape=(
            jax.ShapeDtypeStruct((specs, rows, chans, cols), BF16),
            jax.ShapeDtypeStruct((1, specs), F32),
        ),
        in_specs=[vmem, vmem],
        out_specs=(hbm, hbm),
        scratch_shapes=[dma((specs + 1,))],
        compiler_params=pltpu.CompilerParams(vmem_limit_bytes=1024 * 1024),
        name="store",
    )(*(pltpu.with_memory_space_constraint(x, pltpu.VMEM) for x in (out, bounds)))
    return jnp.transpose(out, (0, 1, 3, 2)), bounds.reshape(specs)


def solution(mesh):
    in_specs = (
        P("rows", None, None),
        P("rows", None, None),
        P(),
        P(),
        P("rows", None, None),
        P("specs", "rows", None, None),
        P("specs"),
        P(),
    )
    out_specs = (P("specs", "rows", None, None), P("specs"))
    return jax.shard_map(
        per_device, mesh=mesh, in_specs=in_specs, out_specs=out_specs, check_vma=False
    )
```

```python
import functools

import jax
import jax.numpy as jnp
from jax import lax
from jax.experimental import pallas as pl
from jax.experimental.pallas import tpu as pltpu
from jax.sharding import PartitionSpec as P

F32 = jnp.float32
BF16 = jnp.bfloat16
MESH = pl.DeviceIdType.MESH


def split2(value):
    high = value.astype(BF16)
    return high, (value - high.astype(F32)).astype(BF16)


def combine(first, middle, last):
    width = first.shape[1]
    rolled = pltpu.roll(first, 1, 1)
    lane = lax.broadcasted_iota(jnp.int32, (first.shape[0], 128), 1)
    rolled = jnp.concatenate(
        [jnp.where(lane == 0, 0.0, rolled[:, :128]), rolled[:, 128:]], axis=1
    )
    back = pltpu.roll(last, width - 1, 1)
    back = jnp.concatenate(
        [back[:, :-128], jnp.where(lane == 127, 0.0, back[:, -128:])], axis=1
    )
    return rolled + middle + back


def fold(value):
    rows, width = value.shape
    return jnp.sum(value.reshape(rows // 8, 8, width), axis=0)


def kernel(
    n_rows,
    center_hbm, radius_hbm, weight_hbm, bias_hbm, status_hbm, coeff_hbm, ids_hbm, table_hbm,
    out_ref, bounds_ref,
    center, radius, status, coeff, weight_ref, bias_ref, ids_ref, table_ref,
    low_end, high_end, slopes, icept, edge_slopes,
    box_edge, halo_box, halo_coeff, shifted, box_weight, rad_weight, back_weight, edge_weight, bias_col,
    acc, parts, table_vec,
    load_sem, coeff_sem, box_send, box_recv, pass_send, pass_recv,
    slope_send, slope_recv, spass_send, spass_recv, row_send, row_recv, part_send, part_recv,
):
    specs, rows, chans, cols = coeff.shape
    half = chans // 2
    me = lax.axis_index("rows")
    lane_dev = lax.axis_index("specs")
    core = lax.rem(lane_dev, 2)
    partner = lane_dev + 1 - 2 * core
    has_prev = me > 0
    has_next = me < n_rows - 1
    mine = pl.ds(pl.multiple_of(core * half, half), half)
    exists = (has_prev, has_next)
    sends = (has_next, has_prev)
    target = (me + 1, me - 1)
    sent_row = (rows - 1, 0)

    loads = [
        pltpu.make_async_copy(center_hbm, center.at[pl.ds(1, rows)], load_sem.at[0]),
        pltpu.make_async_copy(radius_hbm, radius.at[pl.ds(1, rows)], load_sem.at[1]),
        pltpu.make_async_copy(status_hbm, status, load_sem.at[2]),
    ]
    small = [
        pltpu.make_async_copy(weight_hbm, weight_ref, load_sem.at[3]),
        pltpu.make_async_copy(bias_hbm, bias_ref, load_sem.at[4]),
        pltpu.make_async_copy(ids_hbm, ids_ref, load_sem.at[5]),
        pltpu.make_async_copy(table_hbm, table_ref, load_sem.at[6]),
    ]
    for copy in loads[:2] + small + loads[2:]:
        copy.start()

    barrier = pltpu.get_barrier_semaphore()
    for step in range(1, n_rows):
        pl.semaphore_signal(
            barrier, inc=1, device_id={"rows": lax.rem(me + step, n_rows)}, device_id_type=MESH
        )
    pl.semaphore_signal(barrier, inc=1, device_id={"specs": partner}, device_id_type=MESH)

    for copy in loads[:2]:
        copy.wait()
    for d in range(2):
        for a, ref in enumerate((center, radius)):
            box_edge[d, a] = ref[1 + sent_row[d]].astype(BF16)
    pl.semaphore_wait(barrier, n_rows)

    def box_copy(d):
        return pltpu.make_async_remote_copy(
            src_ref=box_edge.at[d, :, mine],
            dst_ref=halo_box.at[d, :, mine],
            send_sem=box_send.at[d],
            recv_sem=box_recv.at[d],
            device_id={"rows": target[d]},
            device_id_type=MESH,
        )

    def pass_copy(d):
        return pltpu.make_async_remote_copy(
            src_ref=halo_box.at[d, :, mine],
            dst_ref=halo_box.at[d, :, mine],
            send_sem=pass_send.at[d],
            recv_sem=pass_recv.at[d],
            device_id={"specs": partner},
            device_id_type=MESH,
        )

    def slope_copy(d):
        return pltpu.make_async_remote_copy(
            src_ref=slopes.at[sent_row[d], mine],
            dst_ref=edge_slopes.at[d, mine],
            send_sem=slope_send.at[d],
            recv_sem=slope_recv.at[d],
            device_id={"rows": target[d]},
            device_id_type=MESH,
        )

    def spass_copy(d):
        return pltpu.make_async_remote_copy(
            src_ref=edge_slopes.at[d, mine],
            dst_ref=edge_slopes.at[d, mine],
            send_sem=spass_send.at[d],
            recv_sem=spass_recv.at[d],
            device_id={"specs": partner},
            device_id_type=MESH,
        )

    def row_copy(d, s):
        return pltpu.make_async_remote_copy(
            src_ref=coeff_hbm.at[s, sent_row[d]],
            dst_ref=halo_coeff.at[d, s],
            send_sem=row_send.at[d, s],
            recv_sem=row_recv.at[d, s],
            device_id={"rows": target[d]},
            device_id_type=MESH,
        )

    first = specs // 2
    for d in range(2):
        @pl.when(sends[d])
        def _():
            box_copy(d).start()
            for s in range(first):
                row_copy(d, s).start()

    coeff_loads = [
        pltpu.make_async_copy(coeff_hbm.at[s], coeff.at[s], coeff_sem.at[s]) for s in range(specs)
    ]
    for copy in coeff_loads:
        copy.start()

    for d in range(2):
        @pl.when(jnp.logical_not(exists[d]))
        def _():
            halo_box[d] = jnp.zeros(halo_box.shape[1:], BF16)

    for copy in small:
        copy.wait()

    zeros = jnp.zeros((chans, chans), F32)
    back = jnp.concatenate([weight_ref[2 - k, j] for k in range(3) for j in range(3)], axis=1)
    blank3 = jnp.zeros((chans, 3 * chans), F32)
    upper_rows = jnp.concatenate([back, blank3], axis=1).astype(BF16)
    lower_rows = jnp.concatenate([blank3, back], axis=1).astype(BF16)
    bias_row = bias_ref[...]
    bias_high = bias_row.astype(BF16).astype(F32)
    bias_mid = (bias_row - bias_high).astype(BF16).astype(F32)
    bias_low = bias_row - bias_high - bias_mid
    zrow = jnp.zeros((1, chans), F32)
    bias_parts = (bias_high, bias_mid, bias_low)

    def bias_rows(own):
        lines = [
            jnp.concatenate(
                [part if k in own and j == 1 else zrow for k in range(4) for j in range(3)], axis=1
            )
            for part in bias_parts
        ]
        return jnp.concatenate(lines + [jnp.zeros((13, 12 * chans), F32)], axis=0).astype(BF16)

    back_weight[...] = jnp.concatenate([upper_rows, lower_rows, bias_rows((1, 2))], axis=0)
    edge = jnp.concatenate(
        [
            jnp.concatenate([weight_ref[2 - k, 2 - j] for k in range(3)] + [zeros], axis=1)
            for j in range(3)
        ],
        axis=0,
    )
    for d, block in ((0, edge), (1, pltpu.roll(edge, chans, 1))):
        lines = [
            jnp.concatenate([part if k == 1 + d else zrow for k in range(4)], axis=1)
            for part in bias_parts
        ]
        lines.append(jnp.zeros((13, 4 * chans), F32))
        edge_weight[d] = jnp.concatenate([block] + lines, axis=0).astype(BF16)

    wide = jnp.concatenate(
        [
            jnp.concatenate([weight_ref[k, j] for j in range(3)] + [zeros], axis=1)
            for k in range(3)
        ]
        + [jnp.zeros((chans, 4 * chans), F32)],
        axis=0,
    )
    fore = wide.T[: 3 * chans]
    fore = jnp.concatenate([fore, pltpu.roll(fore, chans, 1)], axis=0)
    high, low = split2(fore)
    box_weight[...] = jnp.concatenate([high, low, high], axis=1)
    rad_weight[...] = jnp.abs(fore).astype(BF16)

    eye = lax.broadcasted_iota(jnp.int32, (chans, chans), 0) == lax.broadcasted_iota(
        jnp.int32, (chans, chans), 1
    )
    bias_col[...] = jnp.broadcast_to(
        jnp.sum(jnp.where(eye, jnp.broadcast_to(bias_row, (chans, chans)), 0.0), axis=1, keepdims=True),
        (chans, 128),
    )

    where_in_table = (
        lax.broadcasted_iota(jnp.int32, table_ref.shape, 0) * 128
        + lax.broadcasted_iota(jnp.int32, table_ref.shape, 1)
    )
    for s in range(specs):
        table_vec[pl.ds(s, 1), :] = jnp.sum(
            jnp.where(where_in_table == ids_ref[s], table_ref[...], 0.0), axis=0, keepdims=True
        )

    def field(four_rows, weight):
        high, low = split2(four_rows)
        return jnp.dot(
            weight, jnp.concatenate([high, high, low], axis=0), preferred_element_type=F32
        )

    def plain(four_rows, weight):
        return jnp.dot(weight, four_rows.astype(BF16), preferred_element_type=F32)

    def relax(h, c_res, r_res):
        blocks = [slice(j * chans, (j + 1) * chans) for j in range(3)]
        center_out = combine(*(c_res[b] for b in blocks)) + bias_col[:, :1]
        radius_out = combine(*(r_res[b] for b in blocks))
        upper = center_out + radius_out
        lower = center_out - radius_out
        spread = 2.0 * radius_out
        relaxed = jnp.minimum(jnp.maximum(upper, 0.0), spread) / spread
        state = status[h]
        slope = jnp.where(state == 2, relaxed, jnp.where(state == 1, 1.0, 0.0))
        slopes[h] = slope.astype(BF16)
        cut = jnp.where(state == 2, -relaxed * jnp.minimum(lower, 0.0), 0.0)
        icept[h] = cut.astype(BF16).astype(F32)
        low_end[h] = center[h + 1] - radius[h + 1]
        high_end[h] = center[h + 1] + radius[h + 1]

    loads[2].wait()
    pairs = (rows - 2) // 2

    def inner_slopes(p):
        h = 1 + 2 * p
        four = lambda ref: ref[pl.ds(h, 4)].reshape(4 * chans, cols)
        c_res = field(four(center), box_weight[...])
        r_res = plain(four(radius), rad_weight[...])
        for r in range(2):
            block = slice(3 * chans * r, 3 * chans * (r + 1))
            relax(h + r, c_res[block], r_res[block])

    inner_slopes(0)
    for d in range(2):
        @pl.when(exists[d])
        def _():
            box_copy(d).wait_recv()
            pass_copy(d).start()
    inner_slopes(1)
    for d in range(2):
        @pl.when(exists[d])
        def _():
            pass_copy(d).wait()

    blank = jnp.zeros((chans, cols), F32)
    for d, ref_row in ((0, 0), (1, rows - 1)):
        def three(a, ref):
            own = [ref[1], ref[2]] if d == 0 else [ref[rows - 1], ref[rows]]
            halo = [halo_box[d, a].astype(F32)]
            return jnp.concatenate((halo + own if d == 0 else own + halo) + [blank], axis=0)

        c_res = field(three(0, center), box_weight[pl.ds(0, 3 * chans)])
        r_res = plain(three(1, radius), rad_weight[pl.ds(0, 3 * chans)])
        relax(ref_row, c_res, r_res)

    for d in range(2):
        @pl.when(sends[d])
        def _():
            slope_copy(d).start()
            for s in range(first, specs):
                row_copy(d, s).start()
    for p in range(2, pairs):
        inner_slopes(p)

    def finish(s, h, value):
        out_ref[s, h] = value.astype(BF16)
        return fold(jnp.minimum(value * low_end[h], value * high_end[h]))

    lane = lax.broadcasted_iota(jnp.int32, (chans, 128), 1)

    def shifts(pre):
        none = jnp.zeros((chans, 128), BF16)
        ahead = pltpu.roll(pre, cols - 1, 1)
        ahead = jnp.concatenate(
            [ahead[:, :-128], jnp.where(lane == 127, none, ahead[:, -128:])], axis=1
        )
        behind = pltpu.roll(pre, 1, 1)
        behind = jnp.concatenate(
            [jnp.where(lane == 0, none, behind[:, :128]), behind[:, 128:]], axis=1
        )
        return ahead, pre, behind

    def edge_row(s, d, halo):
        h = 0 if d == 0 else rows - 1
        own = pl.ds(0, 3) if d == 0 else pl.ds(rows - 3, 3)
        near = shifted[s, own, 1].reshape(3 * chans, cols)
        four = jnp.concatenate([halo, near] if d == 0 else [near, halo], axis=0)
        result = jnp.dot(edge_weight[d], four, preferred_element_type=F32)
        value = combine(*(result[j * chans : (j + 1) * chans] for j in range(3)))
        acc[s] += finish(s, h, value) + fold(result[3 * chans :])

    for copy in coeff_loads:
        copy.wait()

    def inner(s, carry):
        total = jnp.zeros((8, cols), F32)
        for h in range(rows):
            block = coeff[s, h]
            for j, moved in enumerate(shifts(block * slopes[h])):
                shifted[s, h, j] = moved
            total += fold(jnp.minimum(block, 0).astype(F32) * icept[h])
        for p in range(pairs):
            h = 1 + 2 * p
            pre = shifted[s, pl.ds(h - 1, 4)].reshape(12 * chans, cols)
            result = jnp.dot(back_weight[...], pre, preferred_element_type=F32)
            for r in range(2):
                total += finish(s, h + r, result[chans * r : chans * (r + 1)])
            total += fold(result[2 * chans :])
        acc[s] = total
        return carry

    lax.fori_loop(0, specs // 2, inner, 0)
    for d in range(2):
        @pl.when(exists[d])
        def _():
            slope_copy(d).wait_recv()
            spass_copy(d).start()
    lax.fori_loop(specs // 2, specs, inner, 0)

    for d in range(2):
        @pl.when(jnp.logical_not(exists[d]))
        def _():
            def at_border(s, carry):
                edge_row(s, d, jnp.zeros((chans, cols), BF16))
                return carry

            lax.fori_loop(0, specs, at_border, 0)

    for d in range(2):
        @pl.when(exists[d])
        def _():
            spass_copy(d).wait()

            def at_halo(s, carry):
                row_copy(d, s).wait_recv()
                edge_row(s, d, halo_coeff[d, s] * edge_slopes[d])
                return carry

            lax.fori_loop(0, specs, at_halo, 0)

    folded = jnp.sum(acc[...], axis=1)
    share = folded[:, :128]
    for t in range(1, cols // 128):
        share += folded[:, 128 * t : 128 * (t + 1)]
    parts[0] = share

    def part_copy(step):
        return pltpu.make_async_remote_copy(
            src_ref=parts.at[0],
            dst_ref=parts.at[step],
            send_sem=part_send.at[step],
            recv_sem=part_recv.at[step],
            device_id={"rows": lax.rem(me + step, n_rows)},
            device_id_type=MESH,
        )

    for step in range(1, n_rows):
        part_copy(step).start()
    for d in range(2):
        @pl.when(sends[d])
        def _():
            box_copy(d).wait_send()
            slope_copy(d).wait_send()
            for s in range(specs):
                row_copy(d, s).wait_send()
    for step in range(1, n_rows):
        part_copy(step).wait()
    total = parts[0]
    for step in range(1, n_rows):
        total += parts[step]
    bound = jnp.sum(
        total * (1.0 / (rows * n_rows * cols)) + table_vec[...], axis=1, keepdims=True
    )
    shape = (specs, 128)
    diagonal = lax.broadcasted_iota(jnp.int32, shape, 0) == lax.broadcasted_iota(
        jnp.int32, shape, 1
    )
    line = jnp.sum(jnp.where(diagonal, jnp.broadcast_to(bound, shape), 0.0), axis=0, keepdims=True)
    bounds_ref[...] = line[:, :specs]


def store_kernel(out_vmem, bounds_vmem, out_hbm, bounds_hbm, sem):
    specs = out_vmem.shape[0]
    copies = [
        pltpu.make_async_copy(out_vmem.at[s], out_hbm.at[s], sem.at[s]) for s in range(specs)
    ]
    copies.append(pltpu.make_async_copy(bounds_vmem, bounds_hbm, sem.at[specs]))
    for copy in copies:
        copy.start()
    for copy in copies:
        copy.wait()


def per_device(
    center, radius, conv_weight, conv_bias, split_status, out_coeffs, spec_ids, spec_offsets
):
    n_rows = lax.axis_size("rows")
    specs, rows, cols, chans = out_coeffs.shape
    swap3 = lambda x: jnp.transpose(x, (0, 2, 1))
    dma = pltpu.SemaphoreType.DMA
    vmem = pl.BlockSpec(memory_space=pltpu.VMEM)
    out, bounds = pl.pallas_call(
        functools.partial(kernel, n_rows),
        out_shape=(
            pltpu.VMEM((specs, rows, chans, cols), BF16),
            pltpu.VMEM((1, specs), F32),
        ),
        in_specs=[
            pl.BlockSpec(memory_space=pltpu.HBM),
        ] * 8,
        out_specs=(vmem, vmem),
        scratch_shapes=[
            pltpu.VMEM((rows + 2, chans, cols), F32),
            pltpu.VMEM((rows + 2, chans, cols), F32),
            pltpu.VMEM((rows, chans, cols), jnp.int32),
            pltpu.VMEM((specs, rows, chans, cols), BF16),
            pltpu.VMEM(conv_weight.shape, F32),
            pltpu.VMEM((1, chans), F32),
            pltpu.SMEM((specs,), jnp.int32),
            pltpu.VMEM((spec_offsets.shape[0] // 128, 128), F32),
            pltpu.VMEM((rows, chans, cols), F32),
            pltpu.VMEM((rows, chans, cols), F32),
            pltpu.VMEM((rows, chans, cols), BF16),
            pltpu.VMEM((rows, chans, cols), F32),
            pltpu.VMEM((2, chans, cols), BF16),
            pltpu.VMEM((2, 2, chans, cols), BF16),
            pltpu.VMEM((2, 2, chans, cols), BF16),
            pltpu.VMEM((2, specs, chans, cols), BF16),
            pltpu.VMEM((specs, rows, 3, chans, cols), BF16),
            pltpu.VMEM((6 * chans, 12 * chans), BF16),
            pltpu.VMEM((6 * chans, 4 * chans), BF16),
            pltpu.VMEM((2 * chans + 16, 12 * chans), BF16),
            pltpu.VMEM((2, 3 * chans + 16, 4 * chans), BF16),
            pltpu.VMEM((chans, 128), F32),
            pltpu.VMEM((specs, 8, cols), F32),
            pltpu.VMEM((n_rows, specs, 128), F32),
            pltpu.VMEM((specs, 128), F32),
            dma((7,)), dma((specs,)),
            dma((2,)), dma((2,)), dma((2,)), dma((2,)),
            dma((2,)), dma((2,)), dma((2,)), dma((2,)),
            dma((2, specs)), dma((2, specs)), dma((n_rows,)), dma((n_rows,)),
        ],
        compiler_params=pltpu.CompilerParams(
            collective_id=0, has_side_effects=True, vmem_limit_bytes=48 * 1024 * 1024
        ),
        name="bound_pass",
    )(
        *(
            pltpu.with_memory_space_constraint(x, pltpu.HBM)
            for x in (
                swap3(center),
                swap3(radius),
                conv_weight,
                conv_bias.reshape(1, chans),
                swap3(split_status),
                jnp.transpose(out_coeffs, (0, 1, 3, 2)),
                spec_ids,
                spec_offsets.reshape(-1, 128),
            )
        )
    )
    hbm = pl.BlockSpec(memory_space=pltpu.HBM)
    out, bounds = pl.pallas_call(
        store_kernel,
        out_shape=(
            jax.ShapeDtypeStruct((specs, rows, chans, cols), BF16),
            jax.ShapeDtypeStruct((1, specs), F32),
        ),
        in_specs=[vmem, vmem],
        out_specs=(hbm, hbm),
        scratch_shapes=[dma((specs + 1,))],
        compiler_params=pltpu.CompilerParams(vmem_limit_bytes=1024 * 1024),
        name="store",
    )(*(pltpu.with_memory_space_constraint(x, pltpu.VMEM) for x in (out, bounds)))
    return jnp.transpose(out, (0, 1, 3, 2)), bounds.reshape(specs)


def solution(mesh):
    in_specs = (
        P("rows", None, None),
        P("rows", None, None),
        P(),
        P(),
        P("rows", None, None),
        P("specs", "rows", None, None),
        P("specs"),
        P(),
    )
    out_specs = (P("specs", "rows", None, None), P("specs"))
    return jax.shard_map(
        per_device, mesh=mesh, in_specs=in_specs, out_specs=out_specs, check_vma=False
    )
```
